32 devices in a mesh: trk: 8 (over z, x), frm: 4 (over y, core).
Axes of the slice: x: 2, y: 2, z: 4, core: 2. Of those that a mesh axis runs over, the one named last changes fastest.
Arguments:
- tokens: bfloat16 [256, 32, 384], P('trk', 'frm'), may hold values from -10 to 10
- visible: int32 [256, 32], P('trk', 'frm'), may hold values from 0 to 1, as said below
- virtual: bfloat16 [64, 32, 384], P(None, 'frm'), may hold values from -10 to 10
- time_qkv: bfloat16 [384, 1152], replicated, may hold values from -2 to 2
- time_out: bfloat16 [384, 384], replicated, may hold values from -0.3125 to 0.3125
- virt_q: bfloat16 [384, 384], replicated, may hold values from -2 to 2
- virt_kv: bfloat16 [384, 768], replicated, may hold values from -2 to 2
- virt_out: bfloat16 [384, 384], replicated, may hold values from -0.3125 to 0.3125
- self_qkv: bfloat16 [384, 1152], replicated, may hold values from -2 to 2
- self_out: bfloat16 [384, 384], replicated, may hold values from -0.3125 to 0.3125
- back_q: bfloat16 [384, 384], replicated, may hold values from -2 to 2
- back_kv: bfloat16 [384, 768], replicated, may hold values from -2 to 2
- back_out: bfloat16 [384, 384], replicated, may hold values from -0.3125 to 0.3125
Outputs:
- tracks_out: bfloat16 [256, 32, 384], P('trk', 'frm')
- virtual_out: bfloat16 [64, 32, 384], P(None, 'frm')
The draws below stay inside these ranges and needn't reach their ends.
Inputs may be any that keep to these rules, and one draw needn't show every extreme that they name: 1 where the track is visible in the frame, else 0; in every frame at least one track is visible.
All inputs are finite; a program needn't handle non-finite values.
Results may differ from the reference program's by a relative error of at most 0.015.
Values may be sent and summed in bfloat16 or wider, within the bound.
A program may use at most 384 MiB of HBM per device.

```python
import math
import jax
import jax.numpy as jnp
from jax import lax

D = 384
HEADS = 8
VIRT = 64
FRAMES = 32
TRACKS = 256


def drawn_weight(key, row_count, col_count):
    return jnp.clip(jax.random.normal(key, (row_count, col_count), jnp.float32), -6.0, 6.0) * D ** (-0.5)


def draw_tokens(key, part):
    key = jax.random.fold_in(key, 21)
    first = jax.random.fold_in(key, 0)
    shape_all = (TRACKS, FRAMES, D)
    values = jnp.clip(jax.random.normal(first, shape_all, jnp.float32), -6.0, 6.0)
    return values.astype(jnp.bfloat16)


def draw_virtual(key, part):
    key = jax.random.fold_in(key, 23)
    first = jax.random.fold_in(key, 0)
    shape_all = (VIRT, FRAMES, D)
    values = jnp.clip(jax.random.normal(first, shape_all, jnp.float32), -6.0, 6.0)
    return values.astype(jnp.bfloat16)


def draw_visible(key, part):
    key = jax.random.fold_in(key, 31)
    first, second = jax.random.split(key, 2)
    seen_draw = jax.random.randint(first, (TRACKS, FRAMES), 0, 4) < 3
    picked = jax.random.randint(second, (FRAMES,), 0, TRACKS)
    forced = jnp.arange(TRACKS)[:, None] == picked[None, :]
    return jnp.logical_or(seen_draw, forced).astype(jnp.int32)


def draw_time_qkv(key, part):
    key = jax.random.fold_in(key, 41)
    matrix = drawn_weight(key, D, 3 * D)
    return matrix.astype(jnp.bfloat16)


def draw_virt_q(key, part):
    key = jax.random.fold_in(key, 43)
    matrix = drawn_weight(key, D, D)
    return matrix.astype(jnp.bfloat16)


def draw_virt_kv(key, part):
    key = jax.random.fold_in(key, 47)
    matrix = drawn_weight(key, D, 2 * D)
    return matrix.astype(jnp.bfloat16)


def draw_self_qkv(key, part):
    key = jax.random.fold_in(key, 53)
    matrix = drawn_weight(key, D, 3 * D)
    return matrix.astype(jnp.bfloat16)


def draw_back_q(key, part):
    key = jax.random.fold_in(key, 59)
    matrix = drawn_weight(key, D, D)
    return matrix.astype(jnp.bfloat16)


def draw_back_kv(key, part):
    key = jax.random.fold_in(key, 61)
    matrix = drawn_weight(key, D, 2 * D)
    return matrix.astype(jnp.bfloat16)


def gaussian(rng, dims, width, limit, held_as=jnp.bfloat16):
    entries = width * jax.random.normal(rng, dims, jnp.float32)
    return jnp.clip(entries, min=-limit, max=limit).astype(held_as)


def setup_inputs(seed: int = 0) -> dict:
    streams_of = jax.random.split(jax.random.key(seed), 14)
    tokens = draw_tokens(jax.random.fold_in(streams_of[13], 71), 0)
    visible = draw_visible(jax.random.fold_in(streams_of[13], 71), 0)
    virtual = draw_virtual(jax.random.fold_in(streams_of[13], 71), 0)
    time_qkv = draw_time_qkv(jax.random.fold_in(streams_of[13], 71), 0)
    time_out = gaussian(streams_of[4], (D, D), D ** -0.5, 0.3125)
    virt_q = draw_virt_q(jax.random.fold_in(streams_of[13], 71), 0)
    virt_kv = draw_virt_kv(jax.random.fold_in(streams_of[13], 71), 0)
    virt_out = gaussian(streams_of[7], (D, D), D ** -0.5, 0.3125)
    self_qkv = draw_self_qkv(jax.random.fold_in(streams_of[13], 71), 0)
    self_out = gaussian(streams_of[9], (D, D), D ** -0.5, 0.3125)
    back_q = draw_back_q(jax.random.fold_in(streams_of[13], 71), 0)
    back_kv = draw_back_kv(jax.random.fold_in(streams_of[13], 71), 0)
    back_out = gaussian(streams_of[12], (D, D), D ** -0.5, 0.3125)
    return dict(tokens=tokens, visible=visible, virtual=virtual, time_qkv=time_qkv, time_out=time_out, virt_q=virt_q, virt_kv=virt_kv, virt_out=virt_out, self_qkv=self_qkv, self_out=self_out, back_q=back_q, back_kv=back_kv, back_out=back_out)


EPS = 1e-05
NEG = -1e+30

def normalize(values):
    widened = values.astype(jnp.float32)
    center = lax.optimization_barrier(jnp.mean(widened, -1, keepdims=True))
    shifted = widened - center
    return (shifted * lax.rsqrt(lax.optimization_barrier(jnp.mean(shifted * shifted, -1, keepdims=True)) + EPS)).astype(jnp.bfloat16)

def project(values, weight):
    leading = values.shape[:-1]
    flat = values.reshape(-1, values.shape[-1])
    return jnp.dot(flat, weight, preferred_element_type=jnp.float32).reshape(leading + (weight.shape[1],))

def split_heads(values):
    return values.reshape(values.shape[:-1] + (HEADS, values.shape[-1] // HEADS))

def time_block(rows_in, time_qkv, time_out):
    scaling = (D // HEADS) ** (-0.5)
    projected = project(normalize(rows_in), time_qkv).astype(jnp.bfloat16)
    queries = split_heads(projected[..., :D]).astype(jnp.float32)
    keys_all = split_heads(projected[..., D:2 * D]).astype(jnp.float32)
    values_all = split_heads(projected[..., 2 * D:]).astype(jnp.float32)
    scores = jnp.einsum('bthe,bshe->bhts', queries, keys_all) * scaling
    weights = jax.nn.softmax(scores, -1).astype(jnp.bfloat16)
    mixed = jnp.einsum('bhts,bshe->bthe', weights.astype(jnp.float32), values_all).astype(jnp.bfloat16)
    mixed = mixed.reshape(rows_in.shape)
    return (rows_in.astype(jnp.float32) + project(mixed, time_out)).astype(jnp.bfloat16)

def virtual_self(virt_cross, self_qkv, self_out):
    scaling = (D // HEADS) ** (-0.5)
    self_proj = project(normalize(virt_cross), self_qkv).astype(jnp.bfloat16)
    self_query = split_heads(self_proj[..., :D]).astype(jnp.float32)
    self_keys = split_heads(self_proj[..., D:2 * D]).astype(jnp.float32)
    self_values = split_heads(self_proj[..., 2 * D:]).astype(jnp.float32)
    scores = jnp.einsum('ifhe,jfhe->fhij', self_query, self_keys) * scaling
    self_weights = jax.nn.softmax(scores, -1).astype(jnp.bfloat16)
    self_mixed = jnp.einsum('fhij,jfhe->ifhe', self_weights.astype(jnp.float32), self_values).astype(jnp.bfloat16)
    self_mixed = self_mixed.reshape(virt_cross.shape)
    return (virt_cross.astype(jnp.float32) + project(self_mixed, self_out)).astype(jnp.bfloat16)

def reference(tokens, visible, virtual, time_qkv, time_out, virt_q, virt_kv, virt_out, self_qkv, self_out, back_q, back_kv, back_out):
    scaling = (D // HEADS) ** (-0.5)
    number = tokens.shape[0]
    length = math.gcd(number, 512)
    blocked = tokens.reshape(number // length, length, FRAMES, D)
    updated = lax.map(lambda block_rows: time_block(block_rows, time_qkv, time_out), blocked)
    seen_blocks = visible.reshape(number // length, length, FRAMES)
    virt_norm = normalize(virtual)
    virt_query = split_heads(project(virt_norm, virt_q).astype(jnp.bfloat16)).astype(jnp.float32)

    def absorb(carry, pieces):
        running_peak, denominator, weighted = carry
        track_rows, seen_now = pieces
        key_value = project(normalize(track_rows), virt_kv).astype(jnp.bfloat16)
        real_keys = split_heads(key_value[..., :D]).astype(jnp.float32)
        real_values = split_heads(key_value[..., D:]).astype(jnp.float32)
        scores = jnp.einsum('ifhe,bfhe->fihb', virt_query, real_keys) * scaling
        is_visible = (jnp.transpose(seen_now) > 0)[:, None, None, :]
        scores = jnp.where(is_visible, scores, NEG)
        new_peak = jnp.maximum(running_peak, lax.optimization_barrier(jnp.max(scores, -1)))
        exp_terms = jnp.exp(scores - new_peak[..., None]) * is_visible.astype(jnp.float32)
        factor = jnp.exp(running_peak - new_peak)
        denominator = denominator * factor + lax.optimization_barrier(jnp.sum(exp_terms, -1))
        weighted = weighted * factor[..., None] + jnp.einsum('fihb,bfhe->fihe', exp_terms, real_values)
        return ((new_peak, denominator, weighted), None)
    start = (jnp.full((FRAMES, VIRT, HEADS), NEG, jnp.float32), jnp.zeros((FRAMES, VIRT, HEADS), jnp.float32), jnp.zeros((FRAMES, VIRT, HEADS, D // HEADS), jnp.float32))
    (running_peak, denominator, weighted), unused = lax.scan(absorb, start, (updated, seen_blocks))
    attended = (weighted / denominator[..., None]).astype(jnp.bfloat16).reshape(FRAMES, VIRT, D)
    attended = jnp.transpose(attended, (1, 0, 2))
    virt_cross = (virtual.astype(jnp.float32) + project(attended, virt_out)).astype(jnp.bfloat16)
    virtual_out = virtual_self(virt_cross, self_qkv, self_out)
    back_pair = project(normalize(virtual_out), back_kv).astype(jnp.bfloat16)
    back_keys = split_heads(back_pair[..., :D]).astype(jnp.float32)
    back_values = split_heads(back_pair[..., D:]).astype(jnp.float32)

    def finish(track_rows):
        queries = split_heads(project(normalize(track_rows), back_q).astype(jnp.bfloat16)).astype(jnp.float32)
        scores = jnp.einsum('bfhe,ifhe->bfhi', queries, back_keys) * scaling
        weights = jax.nn.softmax(scores, -1).astype(jnp.bfloat16)
        mixed = jnp.einsum('bfhi,ifhe->bfhe', weights.astype(jnp.float32), back_values).astype(jnp.bfloat16)
        mixed = mixed.reshape(track_rows.shape)
        return (track_rows.astype(jnp.float32) + project(mixed, back_out)).astype(jnp.bfloat16)
    tracks_out = lax.map(finish, updated).reshape(number, FRAMES, D)
    return (tracks_out, virtual_out)
```

```python
import functools
import math

import jax
import jax.numpy as jnp
from jax import lax
from jax.experimental import pallas as pl
from jax.experimental.pallas import tpu as pltpu
from jax.sharding import PartitionSpec as P

HEADS = 8
EPS = 1e-05
NEG = -1e30
LANES = 128
BF16 = jnp.bfloat16
F32 = jnp.float32
MESH = pl.DeviceIdType.MESH


def normalize(values):
    center = jnp.mean(values, -1, keepdims=True)
    shifted = values - center
    return (shifted * lax.rsqrt(jnp.mean(shifted * shifted, -1, keepdims=True) + EPS)).astype(BF16)


def dot(a, b):
    return jnp.dot(a, b, preferred_element_type=F32)


def dot_t(a, b):
    return lax.dot_general(a, b, (((1,), (1,)), ((), ())), preferred_element_type=F32)


def iota(shape, dim):
    return lax.broadcasted_iota(jnp.int32, shape, dim)


def head_mask(width):
    size = width // HEADS
    low = iota((HEADS, width), 0) * size
    lane = iota((HEADS, width), 1)
    return jnp.where((lane >= low) & (lane < low + size), 1.0, 0.0).astype(F32)


def same_head(rows):
    return jnp.where(
        (iota((rows, LANES), 0) & (HEADS - 1)) == (iota((rows, LANES), 1) & (HEADS - 1)), 1.0, 0.0
    ).astype(BF16)


def spread(width, lanes_used):
    size = width // HEADS
    row = iota((LANES, width), 0)
    low = (row & (HEADS - 1)) * size
    lane = iota((LANES, width), 1)
    return jnp.where((row < lanes_used) & (lane >= low) & (lane < low + size), 1.0, 0.0).astype(BF16)


def by_head(x, mask):
    s, width = x.shape
    return (x[:, None, :] * mask[None]).reshape(s * HEADS, width).astype(BF16)


def attend(q, k, v, mask, ends, scale, seen=None):
    width = q.shape[1]
    scores = dot_t(q, by_head(k, mask))
    if seen is not None:
        scores = jnp.where(seen > 0.5, scores, NEG)
    chunks = scores.shape[1] // LANES
    parts = [scores[:, j * LANES : (j + 1) * LANES] for j in range(chunks)]
    peak = functools.reduce(jnp.maximum, parts)
    shift = LANES // 2
    while shift >= HEADS:
        peak = jnp.maximum(peak, pltpu.roll(peak, shift, 1))
        shift //= 2
    terms = jnp.concatenate([jnp.exp2((part - peak) * scale) for part in parts], axis=1)
    if seen is not None:
        terms = jnp.where(seen > 0.5, terms, 0.0)
    both = dot(terms.astype(BF16), jnp.concatenate([by_head(v, mask), ends], axis=1))
    return both[:, :width], peak, both[:, width:]


def divide(sums, denominator, spreader):
    inverse = 1.0 / denominator
    high = inverse.astype(BF16).astype(F32)
    lane = iota(inverse.shape, 1)
    split = jnp.where(lane < HEADS, high, inverse - high).astype(BF16)
    return (sums * dot(split, spreader)).astype(BF16)


def put(ref, rows, values):
    for j in range(ref.shape[0]):
        ref[j, rows, :] = values[:, j * LANES : (j + 1) * LANES]


def take(ref, rows):
    return jnp.concatenate([ref[j, rows, :] for j in range(ref.shape[0])], axis=1)


def kernel(
    sizes,
    tokens_ref, visible_ref, virtual_ref, *rest,
):
    trk_n, frm_n, tracks, frames, virt, width = sizes
    weights_hbm = rest[:10]
    tracks_out, virtual_out = rest[10:12]
    weights = rest[12:22]
    (
        turned, qkv, sums, dens, back_in, updated, pair, virt_rows, virt_query, seen_all,
        send_sum, send_stat, got_sum, got_stat, mine, gathered, back_query, virt_flat,
        w_sem, a_send, a_recv, b_send, b_recv, s_send, s_recv, t_send, t_recv, g_send, g_recv,
    ) = rest[22:]
    time_qkv, time_out, virt_q, virt_kv, virt_out, self_qkv, self_out, back_q, back_kv, back_out = weights
    scale = (width // HEADS) ** (-0.5) * math.log2(math.e)
    me_t = lax.axis_index("trk")
    me_f = lax.axis_index("frm")
    share = tracks // frm_n
    block = share * frames
    span = frm_n * frames
    always = trk_n == frames

    loads = [
        pltpu.make_async_copy(weights_hbm[j], weights[j], w_sem.at[j]) for j in range(10)
    ]
    for load in loads:
        load.start()

    barrier = pltpu.get_barrier_semaphore()
    for k in range(1, frm_n):
        pl.semaphore_signal(
            barrier, inc=1, device_id=(me_t, lax.rem(me_f + k, frm_n)), device_id_type=MESH
        )
    for k in range(1, trk_n):
        pl.semaphore_signal(
            barrier, inc=1, device_id=(lax.rem(me_t + k, trk_n), me_f), device_id_type=MESH
        )

    mask = head_mask(width)
    ends_tracks = same_head(tracks * HEADS)
    ends_virt = same_head(virt * HEADS)
    ends_span = same_head(span * HEADS)
    spread2 = spread(width, 2 * HEADS)

    pl.semaphore_wait(barrier, frm_n + trk_n - 2)

    def rows(index):
        return pl.ds(pl.multiple_of(index * block, block), block)

    def a_copy(k, peer, source):
        return pltpu.make_async_remote_copy(
            src_ref=tokens_ref.at[rows(peer)],
            dst_ref=turned.at[rows(source)],
            send_sem=a_send.at[peer],
            recv_sem=a_recv.at[source],
            device_id=(me_t, peer),
            device_id_type=MESH,
        )

    def b_copy(peer, source):
        return pltpu.make_async_remote_copy(
            src_ref=back_in.at[rows(peer)],
            dst_ref=updated.at[rows(source)],
            send_sem=b_send.at[peer],
            recv_sem=b_recv.at[source],
            device_id=(me_t, peer),
            device_id_type=MESH,
        )

    for k in range(1, frm_n):
        a_copy(k, lax.rem(me_f + k, frm_n), me_f).start()
    turned[rows(me_f), :] = tokens_ref[rows(me_f), :]

    loads[2].wait()
    every = slice(None)
    virtual = virtual_ref[...].astype(F32)
    put(virt_rows, every, virtual)
    put(virt_query, every, dot(normalize(virtual), virt_q[...]))
    repeat = jnp.where(
        iota((tracks, tracks * HEADS), 0) == iota((tracks, tracks * HEADS), 1) // HEADS, 1.0, 0.0
    ).astype(BF16)
    seen_all[...] = lax.dot_general(
        visible_ref[...].astype(F32).astype(BF16),
        repeat,
        (((0,), (0,)), ((), ())),
        preferred_element_type=F32,
    )
    loads[0].wait()
    for k in range(1, frm_n):
        peer = lax.rem(me_f + frm_n - k, frm_n)
        a_copy(k, peer, peer).wait_recv()

    qkv[...] = dot(normalize(turned[...].astype(F32)), time_qkv[...]).reshape(
        frm_n, share, frames, 3 * width
    )
    for n in range(share):
        track = qkv[:, n].reshape(span, 3 * width)
        total, _, den = attend(
            track[:, :width].astype(BF16), track[:, width : 2 * width], track[:, 2 * width :],
            mask, ends_span, scale,
        )
        sums[:, n] = total.reshape(frm_n, frames, width)
        dens[:, n] = den.reshape(frm_n, frames, LANES)
    all_rows = tracks * frames
    mixed = divide(
        sums[...].reshape(all_rows, width), dens[...].reshape(all_rows, LANES), spread2
    )
    loads[1].wait()
    back_in[...] = (turned[...].astype(F32) + dot(mixed, time_out[...])).astype(BF16)
    for k in range(1, frm_n):
        b_copy(lax.rem(me_f + k, frm_n), me_f).start()
    updated[rows(me_f), :] = back_in[rows(me_f), :]
    loads[3].wait()
    loads[7].wait()
    for k in range(1, frm_n):
        peer = lax.rem(me_f + frm_n - k, frm_n)
        b_copy(peer, peer).wait_recv()

    fresh = normalize(updated[...].astype(F32))
    put(pair, every, dot(fresh, virt_kv[...]))
    pack = jnp.where(
        iota((HEADS, LANES), 0) == ((iota((HEADS, LANES), 1) // HEADS) & (HEADS - 1)), 1.0, 0.0
    ).astype(F32)
    groups = virt // HEADS

    def s_copies(frame, source):
        return (
            pltpu.make_async_remote_copy(
                src_ref=send_sum.at[frame], dst_ref=got_sum.at[source],
                send_sem=s_send.at[frame], recv_sem=s_recv.at[source],
                device_id=(frame, me_f), device_id_type=MESH,
            ),
            pltpu.make_async_remote_copy(
                src_ref=send_stat.at[frame], dst_ref=got_stat.at[source],
                send_sem=t_send.at[frame], recv_sem=t_recv.at[source],
                device_id=(frame, me_f), device_id_type=MESH,
            ),
        )

    def remote(frame, step, act):
        if always:
            if step < frames - 1:
                act()
        else:
            pl.when(frame != me_t)(act)

    def send_partial(frame):
        for copy in s_copies(frame, me_t):
            copy.start()

    for step in range(frames):
        frame = lax.rem(me_t + 1 + step, frames)
        both = take(pair, pl.ds(frame, tracks, stride=frames))
        total, peak, den = attend(
            take(virt_query, pl.ds(frame, virt, stride=frames)).astype(BF16),
            both[:, :width], both[:, width:],
            mask, ends_tracks, scale, seen=seen_all[pl.ds(frame, 1), :],
        )
        send_sum[frame] = total.astype(BF16)
        for j, stat in enumerate((peak, den)):
            send_stat[frame, j] = jnp.sum(stat.reshape(groups, HEADS, LANES) * pack[None], axis=1)
        remote(frame, step, functools.partial(send_partial, frame))

    put(back_query, every, dot(fresh, back_q[...]))
    loads[4].wait()
    loads[5].wait()
    loads[6].wait()

    def g_copy(peer, frame):
        return pltpu.make_async_remote_copy(
            src_ref=mine, dst_ref=gathered.at[frame],
            send_sem=g_send.at[peer], recv_sem=g_recv.at[frame],
            device_id=(peer, me_f), device_id_type=MESH,
        )

    def own_frame():
        got_sum[me_t] = send_sum[me_t]
        got_stat[me_t] = send_stat[me_t]
        for k in range(1, trk_n):
            peer = lax.rem(me_t + trk_n - k, trk_n)
            for copy in s_copies(me_t, peer):
                copy.wait_recv()
        peaks = got_stat[:, 0]
        factor = jnp.exp2((peaks - jnp.max(peaks, 0, keepdims=True)) * scale)
        factor = factor / jnp.sum(factor * got_stat[:, 1], 0, keepdims=True)
        spread1 = spread(width, HEADS * HEADS)
        attended = jnp.zeros((virt, width), F32)
        for d in range(trk_n):
            wide = (factor[d][:, None, :] * pack[None]).reshape(virt, LANES).astype(BF16)
            attended += got_sum[d].astype(F32) * dot(wide, spread1)
        rows_here = take(virt_rows, pl.ds(me_t, virt, stride=frames))
        cross = (rows_here + dot(attended.astype(BF16), virt_out[...])).astype(BF16).astype(F32)
        proj = dot(normalize(cross), self_qkv[...])
        total, _, den = attend(
            proj[:, :width].astype(BF16), proj[:, width : 2 * width], proj[:, 2 * width :],
            mask, ends_virt, scale,
        )
        self_mixed = divide(total, den, spread2)
        mine[...] = (cross + dot(self_mixed, self_out[...])).astype(BF16)
        for k in range(1, trk_n):
            g_copy(lax.rem(me_t + k, trk_n), me_t).start()
        gathered[me_t] = mine[...]

    if always:
        own_frame()
    else:
        pl.when(me_t < frames)(own_frame)

    loads[8].wait()
    loads[9].wait()
    dens_flat, sums_flat = virt_flat
    for step in range(frames):
        frame = lax.rem(me_t + frames - step, frames)
        if always:
            if step > 0:
                g_copy(frame, frame).wait_recv()
        else:
            pl.when(frame != me_t)(lambda: g_copy(frame, frame).wait_recv())
        rows_f = gathered[frame].astype(F32)
        put(virt_rows, pl.ds(frame, virt, stride=frames), rows_f)
        back = dot(normalize(rows_f), back_kv[...])
        total, _, den = attend(
            take(back_query, pl.ds(frame, tracks, stride=frames)).astype(BF16),
            back[:, :width], back[:, width:], mask, ends_virt, scale,
        )
        put(sums_flat, pl.ds(frame, tracks, stride=frames), total)
        dens_flat[pl.ds(frame, tracks, stride=frames), :] = den
    back_mixed = divide(take(sums_flat, every), dens_flat[...], spread2)
    tracks_out[...] = (updated[...].astype(F32) + dot(back_mixed, back_out[...])).astype(BF16)
    virtual_out[...] = take(virt_rows, every).astype(BF16)

    for k in range(1, frm_n):
        peer = lax.rem(me_f + k, frm_n)
        a_copy(k, peer, me_f).wait_send()
        b_copy(peer, me_f).wait_send()
    for step in range(frames):
        frame = lax.rem(me_t + 1 + step, frames)

        def left(frame=frame):
            for copy in s_copies(frame, me_t):
                copy.wait_send()

        remote(frame, step, left)

    def own_left():
        for k in range(1, trk_n):
            g_copy(lax.rem(me_t + k, trk_n), me_t).wait_send()

    if always:
        own_left()
    else:
        pl.when(me_t < frames)(own_left)


def on_device(mesh_sizes, tokens, visible, virtual, *weights):
    trk_n, frm_n = mesh_sizes
    tracks, frames, width = tokens.shape
    virt = virtual.shape[0]
    assert trk_n >= frames and tracks % frm_n == 0
    share, span = tracks // frm_n, frm_n * frames
    all_rows, virt_all = tracks * frames, virt * frames
    dma = pltpu.SemaphoreType.DMA
    vmem = pl.BlockSpec(memory_space=pltpu.VMEM)
    scratch = [pltpu.VMEM(w.shape, BF16) for w in weights] + [
        pltpu.VMEM((all_rows, width), BF16),
        pltpu.VMEM((frm_n, share, frames, 3 * width), F32),
        pltpu.VMEM((frm_n, share, frames, width), F32),
        pltpu.VMEM((frm_n, share, frames, LANES), F32),
        pltpu.VMEM((all_rows, width), BF16),
        pltpu.VMEM((all_rows, width), BF16),
        pltpu.VMEM((2 * width // LANES, all_rows, LANES), F32),
        pltpu.VMEM((width // LANES, virt_all, LANES), F32),
        pltpu.VMEM((width // LANES, virt_all, LANES), F32),
        pltpu.VMEM((frames, tracks * HEADS), F32),
        pltpu.VMEM((frames, virt, width), BF16),
        pltpu.VMEM((frames, 2, virt // HEADS, LANES), F32),
        pltpu.VMEM((trk_n, virt, width), BF16),
        pltpu.VMEM((trk_n, 2, virt // HEADS, LANES), F32),
        pltpu.VMEM((virt, width), BF16),
        pltpu.VMEM((frames, virt, width), BF16),
        pltpu.VMEM((width // LANES, all_rows, LANES), F32),
        [pltpu.VMEM((all_rows, LANES), F32), pltpu.VMEM((width // LANES, all_rows, LANES), F32)],
        dma((10,)),
        dma((frm_n,)), dma((frm_n,)), dma((frm_n,)), dma((frm_n,)),
        dma((frames,)), dma((trk_n,)), dma((frames,)), dma((trk_n,)),
        dma((trk_n,)), dma((frames,)),
    ]
    tracks_out, virtual_out = pl.pallas_call(
        functools.partial(kernel, (trk_n, frm_n, tracks, frames, virt, width)),
        out_shape=(
            jax.ShapeDtypeStruct((all_rows, width), BF16),
            jax.ShapeDtypeStruct((virt_all, width), BF16),
        ),
        in_specs=[vmem] * 3 + [pl.BlockSpec(memory_space=pl.ANY)] * 10,
        out_specs=(vmem, vmem),
        scratch_shapes=scratch,
        compiler_params=pltpu.CompilerParams(
            collective_id=0, has_side_effects=True, vmem_limit_bytes=48 * 1024 * 1024
        ),
    )(
        tokens.reshape(all_rows, width), visible, virtual.reshape(virt_all, width), *weights
    )
    return tracks_out.reshape(tokens.shape), virtual_out.reshape(virtual.shape)


def solution(mesh):
    placed = (P("trk", "frm", None), P("trk", "frm"), P(None, "frm", None)) + (P(),) * 10
    return jax.shard_map(
        functools.partial(on_device, (mesh.shape["trk"], mesh.shape["frm"])),
        mesh=mesh,
        in_specs=placed,
        out_specs=(P("trk", "frm", None), P(None, "frm", None)),
        check_vma=False,
    )
```

```python
import functools
import math

import jax
import jax.numpy as jnp
from jax import lax
from jax.experimental import pallas as pl
from jax.experimental.pallas import tpu as pltpu
from jax.sharding import PartitionSpec as P

HEADS = 8
EPS = 1e-05
NEG = -1e30
LANES = 128
BF16 = jnp.bfloat16
F32 = jnp.float32
MESH = pl.DeviceIdType.MESH


def normalize(values):
    center = jnp.mean(values, -1, keepdims=True)
    shifted = values - center
    return (shifted * lax.rsqrt(jnp.mean(shifted * shifted, -1, keepdims=True) + EPS)).astype(BF16)


def dot(a, b):
    return jnp.dot(a, b, preferred_element_type=F32)


def dot_t(a, b):
    return lax.dot_general(a, b, (((1,), (1,)), ((), ())), preferred_element_type=F32)


def iota(shape, dim):
    return lax.broadcasted_iota(jnp.int32, shape, dim)


def head_masks(rows, width):
    size = width // HEADS
    lane = iota((rows, LANES), 1)
    masks = []
    for h in range(HEADS):
        low, row = h * size, []
        for j in range(width // LANES):
            first, last = low - j * LANES, low + size - j * LANES
            if last <= 0 or first >= LANES:
                row.append(None)
            else:
                row.append(jnp.where((lane >= first) & (lane < last), 1.0, 0.0).astype(BF16))
        masks.append(row)
    return masks


def same_head(keys):
    lane = iota((keys, LANES), 1) & (HEADS - 1)
    return jnp.concatenate(
        [jnp.where(lane == h, 1.0, 0.0).astype(BF16) for h in range(HEADS)], axis=0
    )


def spread(width, lanes_used):
    size = width // HEADS
    row = iota((LANES, width), 0)
    low = (row & (HEADS - 1)) * size
    lane = iota((LANES, width), 1)
    return jnp.where((row < lanes_used) & (lane >= low) & (lane < low + size), 1.0, 0.0).astype(BF16)


def by_head(x, masks):
    keys = x.shape[0]
    empty = jnp.zeros((keys, LANES), BF16)
    copies = []
    for row in masks:
        tiles = [
            empty if m is None else x[:, j * LANES : (j + 1) * LANES] * m[:keys]
            for j, m in enumerate(row)
        ]
        copies.append(jnp.concatenate(tiles, axis=1))
    return jnp.concatenate(copies, axis=0)


def attend(q, k, v, masks, ends, scale, seen=None):
    rows, width = q.shape
    keys = k.shape[0]
    scores = dot_t(q, by_head(k.astype(BF16), masks))
    if seen is not None:
        scores = jnp.where(seen > 0.5, scores, NEG)
    per = LANES // keys
    lane = iota((rows, LANES), 1)
    terms, peaks = [], []
    for j in range(scores.shape[1] // LANES):
        part = scores[:, j * LANES : (j + 1) * LANES]
        wide = None
        for i in range(per):
            inside = (lane >= i * keys) & (lane < (i + 1) * keys)
            peak = jnp.max(jnp.where(inside, part, -3e38), axis=1, keepdims=True)
            peaks.append(peak)
            wide = jnp.broadcast_to(peak, part.shape) if i == 0 else jnp.where(inside, peak, wide)
        terms.append(jnp.exp2((part - wide) * scale))
    terms = jnp.concatenate(terms, axis=1)
    if seen is not None:
        terms = jnp.where(seen > 0.5, terms, 0.0)
    both = dot(terms.astype(BF16), jnp.concatenate([by_head(v.astype(BF16), masks), ends], axis=1))
    return both[:, :width], peaks, both[:, width:]


def divide(sums, denominator, spreader):
    inverse = 1.0 / denominator
    high = inverse.astype(BF16).astype(F32)
    lane = iota(inverse.shape, 1)
    split = jnp.where(lane < HEADS, high, inverse - high).astype(BF16)
    return (sums * dot(split, spreader)).astype(BF16)


def put(ref, rows, values):
    for j in range(ref.shape[0]):
        ref[j, rows, :] = values[:, j * LANES : (j + 1) * LANES]


def take(ref, rows):
    return jnp.concatenate([ref[j, rows, :] for j in range(ref.shape[0])], axis=1)


def kernel(
    sizes,
    tokens_hbm, visible_ref, virtual_hbm, *rest,
):
    trk_n, frm_n, tracks, frames, virt, width = sizes
    weights_hbm = rest[:10]
    tracks_out, virtual_out = rest[10:12]
    weights = rest[12:22]
    (
        turned, qkv, sums, dens, back_in, updated, pair, virt_rows, virt_query, seen_all,
        send_sum, send_stat, got_sum, got_stat, mine, gathered, back_query, virt_flat,
        virtual_ref, x_sem, w_sem, a_send, a_recv, b_send, b_recv, s_send, s_recv, t_send, t_recv, g_send, g_recv,
    ) = rest[22:]
    time_qkv, time_out, virt_q, virt_kv, virt_out, self_qkv, self_out, back_q, back_kv, back_out = weights
    scale = (width // HEADS) ** (-0.5) * math.log2(math.e)
    me_t = lax.axis_index("trk")
    me_f = lax.axis_index("frm")
    share = tracks // frm_n
    block = share * frames
    span = frm_n * frames
    always = trk_n == frames

    loads = [
        pltpu.make_async_copy(weights_hbm[j], weights[j], w_sem.at[j]) for j in range(10)
    ]
    load_virtual = pltpu.make_async_copy(virtual_hbm, virtual_ref, x_sem.at[0])
    load_virtual.start()
    for j in (2, 0, 1, 3, 7, 4, 5, 6, 8, 9):
        loads[j].start()

    barrier = pltpu.get_barrier_semaphore()
    for k in range(1, frm_n):
        pl.semaphore_signal(
            barrier, inc=1, device_id=(me_t, lax.rem(me_f + k, frm_n)), device_id_type=MESH
        )
    for k in range(1, trk_n):
        pl.semaphore_signal(
            barrier, inc=1, device_id=(lax.rem(me_t + k, trk_n), me_f), device_id_type=MESH
        )

    mask = head_masks(max(virt, tracks, span), width)
    ends_tracks = same_head(tracks)
    ends_virt = same_head(virt)
    ends_span = same_head(span)
    spread2 = spread(width, 2 * HEADS)

    pl.semaphore_wait(barrier, frm_n + trk_n - 2)

    def rows(index):
        return pl.ds(pl.multiple_of(index * block, block), block)

    def a_copy(k, peer, source):
        return pltpu.make_async_remote_copy(
            src_ref=tokens_hbm.at[rows(peer)],
            dst_ref=turned.at[rows(source)],
            send_sem=a_send.at[peer],
            recv_sem=a_recv.at[source],
            device_id=(me_t, peer),
            device_id_type=MESH,
        )

    def b_copy(peer, source):
        return pltpu.make_async_remote_copy(
            src_ref=back_in.at[rows(peer)],
            dst_ref=updated.at[rows(source)],
            send_sem=b_send.at[peer],
            recv_sem=b_recv.at[source],
            device_id=(me_t, peer),
            device_id_type=MESH,
        )

    own_tokens = pltpu.make_async_copy(
        tokens_hbm.at[rows(me_f)], turned.at[rows(me_f)], x_sem.at[1]
    )
    for k in range(1, frm_n):
        a_copy(k, lax.rem(me_f + k, frm_n), me_f).start()
    own_tokens.start()

    loads[2].wait()
    every = slice(None)
    load_virtual.wait()
    virtual = virtual_ref[...].astype(F32)
    put(virt_rows, every, virtual)
    put(virt_query, every, dot(normalize(virtual), virt_q[...]))
    repeat = jnp.where(
        iota((tracks, tracks * HEADS), 0) == lax.rem(iota((tracks, tracks * HEADS), 1), tracks),
        1.0,
        0.0,
    ).astype(BF16)
    seen_all[...] = dot(visible_ref[...].astype(F32).astype(BF16), repeat)
    loads[0].wait()
    own_tokens.wait()
    for k in range(1, frm_n):
        peer = lax.rem(me_f + frm_n - k, frm_n)
        a_copy(k, peer, peer).wait_recv()

    qkv[...] = dot(normalize(turned[...].astype(F32)), time_qkv[...]).reshape(
        frm_n, share, frames, 3 * width
    )
    for n in range(share):
        track = qkv[:, n].reshape(span, 3 * width)
        total, _, den = attend(
            track[:, :width].astype(BF16), track[:, width : 2 * width], track[:, 2 * width :],
            mask, ends_span, scale,
        )
        sums[:, n] = total.reshape(frm_n, frames, width)
        dens[:, n] = den.reshape(frm_n, frames, LANES)
    all_rows = tracks * frames
    mixed = divide(
        sums[...].reshape(all_rows, width), dens[...].reshape(all_rows, LANES), spread2
    )
    loads[1].wait()
    back_in[...] = (turned[...].astype(F32) + dot(mixed, time_out[...])).astype(BF16)
    for k in range(1, frm_n):
        b_copy(lax.rem(me_f + k, frm_n), me_f).start()
    updated[rows(me_f), :] = back_in[rows(me_f), :]
    loads[3].wait()
    loads[7].wait()
    for k in range(1, frm_n):
        peer = lax.rem(me_f + frm_n - k, frm_n)
        b_copy(peer, peer).wait_recv()

    fresh = normalize(updated[...].astype(F32))
    put(pair, every, dot(fresh, virt_kv[...]))
    pack = jnp.where(
        iota((HEADS, LANES), 0) == ((iota((HEADS, LANES), 1) // HEADS) & (HEADS - 1)), 1.0, 0.0
    ).astype(F32)
    groups = virt // HEADS

    def s_copies(frame, source):
        return (
            pltpu.make_async_remote_copy(
                src_ref=send_sum.at[frame], dst_ref=got_sum.at[source],
                send_sem=s_send.at[frame], recv_sem=s_recv.at[source],
                device_id=(frame, me_f), device_id_type=MESH,
            ),
            pltpu.make_async_remote_copy(
                src_ref=send_stat.at[frame], dst_ref=got_stat.at[source],
                send_sem=t_send.at[frame], recv_sem=t_recv.at[source],
                device_id=(frame, me_f), device_id_type=MESH,
            ),
        )

    def remote(frame, step, act):
        if always:
            if step < frames - 1:
                act()
        else:
            pl.when(frame != me_t)(act)

    def send_partial(frame):
        for copy in s_copies(frame, me_t):
            copy.start()

    for step in range(frames):
        frame = lax.rem(me_t + 1 + step, frames)
        both = take(pair, pl.ds(frame, tracks, stride=frames))
        total, peaks, den = attend(
            take(virt_query, pl.ds(frame, virt, stride=frames)).astype(BF16),
            both[:, :width], both[:, width:],
            mask, ends_tracks, scale, seen=seen_all[pl.ds(frame, 1), :],
        )
        send_sum[frame] = total.astype(BF16)
        head = iota((virt, LANES), 1) & (HEADS - 1)
        peak = functools.reduce(
            lambda wide, h: jnp.where(head == h, peaks[h], wide), range(HEADS), jnp.zeros_like(den)
        )
        for j, stat in enumerate((peak, den)):
            send_stat[frame, j] = jnp.sum(stat.reshape(groups, HEADS, LANES) * pack[None], axis=1)
        remote(frame, step, functools.partial(send_partial, frame))

    put(back_query, every, dot(fresh, back_q[...]))
    loads[4].wait()
    loads[5].wait()
    loads[6].wait()

    def g_copy(peer, frame):
        return pltpu.make_async_remote_copy(
            src_ref=mine, dst_ref=gathered.at[frame],
            send_sem=g_send.at[peer], recv_sem=g_recv.at[frame],
            device_id=(peer, me_f), device_id_type=MESH,
        )

    def own_frame():
        got_sum[me_t] = send_sum[me_t]
        got_stat[me_t] = send_stat[me_t]
        for k in range(1, trk_n):
            peer = lax.rem(me_t + trk_n - k, trk_n)
            for copy in s_copies(me_t, peer):
                copy.wait_recv()
        peaks = got_stat[:, 0]
        factor = jnp.exp2((peaks - jnp.max(peaks, 0, keepdims=True)) * scale)
        factor = factor / jnp.sum(factor * got_stat[:, 1], 0, keepdims=True)
        spread1 = spread(width, HEADS * HEADS)
        attended = jnp.zeros((virt, width), F32)
        for d in range(trk_n):
            wide = (factor[d][:, None, :] * pack[None]).reshape(virt, LANES).astype(BF16)
            attended += got_sum[d].astype(F32) * dot(wide, spread1)
        rows_here = take(virt_rows, pl.ds(me_t, virt, stride=frames))
        cross = (rows_here + dot(attended.astype(BF16), virt_out[...])).astype(BF16).astype(F32)
        proj = dot(normalize(cross), self_qkv[...])
        total, _, den = attend(
            proj[:, :width].astype(BF16), proj[:, width : 2 * width], proj[:, 2 * width :],
            mask, ends_virt, scale,
        )
        self_mixed = divide(total, den, spread2)
        mine[...] = (cross + dot(self_mixed, self_out[...])).astype(BF16)
        for k in range(1, trk_n):
            g_copy(lax.rem(me_t + k, trk_n), me_t).start()
        gathered[me_t] = mine[...]

    if always:
        own_frame()
    else:
        pl.when(me_t < frames)(own_frame)

    loads[8].wait()
    loads[9].wait()
    dens_flat, sums_flat = virt_flat
    for step in range(frames):
        frame = lax.rem(me_t + frames - step, frames)
        if always:
            if step > 0:
                g_copy(frame, frame).wait_recv()
        else:
            pl.when(frame != me_t)(lambda: g_copy(frame, frame).wait_recv())
        rows_f = gathered[frame].astype(F32)
        put(virt_rows, pl.ds(frame, virt, stride=frames), rows_f)
        back = dot(normalize(rows_f), back_kv[...])
        total, _, den = attend(
            take(back_query, pl.ds(frame, tracks, stride=frames)).astype(BF16),
            back[:, :width], back[:, width:], mask, ends_virt, scale,
        )
        put(sums_flat, pl.ds(frame, tracks, stride=frames), total)
        dens_flat[pl.ds(frame, tracks, stride=frames), :] = den
    back_mixed = divide(take(sums_flat, every), dens_flat[...], spread2)
    tracks_out[...] = (updated[...].astype(F32) + dot(back_mixed, back_out[...])).astype(BF16)
    virtual_out[...] = take(virt_rows, every).astype(BF16)

    for k in range(1, frm_n):
        peer = lax.rem(me_f + k, frm_n)
        a_copy(k, peer, me_f).wait_send()
        b_copy(peer, me_f).wait_send()
    for step in range(frames):
        frame = lax.rem(me_t + 1 + step, frames)

        def left(frame=frame):
            for copy in s_copies(frame, me_t):
                copy.wait_send()

        remote(frame, step, left)

    def own_left():
        for k in range(1, trk_n):
            g_copy(lax.rem(me_t + k, trk_n), me_t).wait_send()

    if always:
        own_left()
    else:
        pl.when(me_t < frames)(own_left)


def on_device(mesh_sizes, tokens, visible, virtual, *weights):
    trk_n, frm_n = mesh_sizes
    tracks, frames, width = tokens.shape
    virt = virtual.shape[0]
    assert trk_n >= frames and tracks % frm_n == 0
    share, span = tracks // frm_n, frm_n * frames
    all_rows, virt_all = tracks * frames, virt * frames
    dma = pltpu.SemaphoreType.DMA
    vmem = pl.BlockSpec(memory_space=pltpu.VMEM)
    hbm = pl.BlockSpec(memory_space=pltpu.HBM)
    scratch = [pltpu.VMEM(w.shape, BF16) for w in weights] + [
        pltpu.VMEM((all_rows, width), BF16),
        pltpu.VMEM((frm_n, share, frames, 3 * width), F32),
        pltpu.VMEM((frm_n, share, frames, width), F32),
        pltpu.VMEM((frm_n, share, frames, LANES), F32),
        pltpu.VMEM((all_rows, width), BF16),
        pltpu.VMEM((all_rows, width), BF16),
        pltpu.VMEM((2 * width // LANES, all_rows, LANES), F32),
        pltpu.VMEM((width // LANES, virt_all, LANES), F32),
        pltpu.VMEM((width // LANES, virt_all, LANES), F32),
        pltpu.VMEM((frames, tracks * HEADS), F32),
        pltpu.VMEM((frames, virt, width), BF16),
        pltpu.VMEM((frames, 2, virt // HEADS, LANES), F32),
        pltpu.VMEM((trk_n, virt, width), BF16),
        pltpu.VMEM((trk_n, 2, virt // HEADS, LANES), F32),
        pltpu.VMEM((virt, width), BF16),
        pltpu.VMEM((frames, virt, width), BF16),
        pltpu.VMEM((width // LANES, all_rows, LANES), F32),
        [pltpu.VMEM((all_rows, LANES), F32), pltpu.VMEM((width // LANES, all_rows, LANES), F32)],
        pltpu.VMEM((virt_all, width), BF16),
        dma((2,)),
        dma((10,)),
        dma((frm_n,)), dma((frm_n,)), dma((frm_n,)), dma((frm_n,)),
        dma((frames,)), dma((trk_n,)), dma((frames,)), dma((trk_n,)),
        dma((trk_n,)), dma((frames,)),
    ]
    tracks_out, virtual_out = pl.pallas_call(
        functools.partial(kernel, (trk_n, frm_n, tracks, frames, virt, width)),
        out_shape=(
            jax.ShapeDtypeStruct((all_rows, width), BF16),
            jax.ShapeDtypeStruct((virt_all, width), BF16),
        ),
        in_specs=[hbm, vmem, hbm] + [hbm] * 10,
        out_specs=(vmem, vmem),
        scratch_shapes=scratch,
        compiler_params=pltpu.CompilerParams(
            collective_id=0, has_side_effects=True, vmem_limit_bytes=64 * 1024 * 1024
        ),
    )(
        tokens.reshape(all_rows, width), jnp.transpose(visible), virtual.reshape(virt_all, width), *weights
    )
    return tracks_out.reshape(tokens.shape), virtual_out.reshape(virtual.shape)


def solution(mesh):
    placed = (P("trk", "frm", None), P("trk", "frm"), P(None, "frm", None)) + (P(),) * 10
    return jax.shard_map(
        functools.partial(on_device, (mesh.shape["trk"], mesh.shape["frm"])),
        mesh=mesh,
        in_specs=placed,
        out_specs=(P("trk", "frm", None), P(None, "frm", None)),
        check_vma=False,
    )
```

```python
import functools
import math

import jax
import jax.numpy as jnp
from jax import lax
from jax.experimental import pallas as pl
from jax.experimental.pallas import tpu as pltpu
from jax.sharding import PartitionSpec as P

HEADS = 8
HALF = HEADS // 2
EPS = 1e-05
NEG = -1e30
LANES = 128
BF16 = jnp.bfloat16
F32 = jnp.float32
MESH = pl.DeviceIdType.MESH


def normalize(values):
    center = jnp.mean(values, -1, keepdims=True)
    shifted = values - center
    return (shifted * lax.rsqrt(jnp.mean(shifted * shifted, -1, keepdims=True) + EPS)).astype(BF16)


def dot(a, b):
    return jnp.dot(a, b, preferred_element_type=F32)


def dot_t(a, b):
    return lax.dot_general(a, b, (((1,), (1,)), ((), ())), preferred_element_type=F32)


def iota(shape, dim):
    return lax.broadcasted_iota(jnp.int32, shape, dim)


def head_masks(rows, width):
    size = width // HEADS
    lane = iota((rows, LANES), 1)
    masks = []
    for h in range(HEADS):
        low, row = h * size, []
        for j in range(width // LANES):
            first, last = low - j * LANES, low + size - j * LANES
            if last <= 0 or first >= LANES:
                row.append(None)
            else:
                row.append(jnp.where((lane >= first) & (lane < last), 1.0, 0.0).astype(BF16))
        masks.append(row)
    return masks


def spread(width, lanes_used):
    size = width // HEADS
    row = iota((LANES, width), 0)
    low = (row & (HEADS - 1)) * size
    lane = iota((LANES, width), 1)
    return jnp.where((row < lanes_used) & (lane >= low) & (lane < low + size), 1.0, 0.0).astype(BF16)


def by_head(x, masks, group, totals=False):
    keys = x.shape[0]
    lane = iota((keys, LANES), 1)
    free = lane >= LANES // 2 if group == 0 else lane < LANES // 2
    copies = []
    for h in range(group * HALF, (group + 1) * HALF):
        tiles = []
        for j in (group, group + 1):
            m = masks[h][j]
            tile = jnp.zeros((keys, LANES), BF16)
            if m is not None:
                tile = x[:, j * LANES : (j + 1) * LANES] * m[:keys]
            if totals and j == 1:
                ones = jnp.where(free & ((lane & (HEADS - 1)) == h), 1.0, 0.0).astype(BF16)
                tile = ones if m is None else tile + ones
            tiles.append(tile)
        copies.append(jnp.concatenate(tiles, axis=1))
    return jnp.concatenate(copies, axis=0)


def attend(q, k, v, masks, scale, seen=None):
    rows = q.shape[0]
    keys = k.shape[0]
    k, v = k.astype(BF16), v.astype(BF16)
    per = LANES // keys
    lane = iota((rows, LANES), 1)
    peaks, outs = [], []
    for group in range(2):
        window = slice(group * LANES, (group + 2) * LANES)
        scores = dot_t(q[:, window], by_head(k, masks, group))
        terms = []
        for j in range(HALF * keys // LANES):
            part = scores[:, j * LANES : (j + 1) * LANES]
            if seen is not None:
                part = jnp.where(seen > 0.5, part, NEG)
            wide = None
            for i in range(per):
                inside = (lane >= i * keys) & (lane < (i + 1) * keys)
                peak = jnp.max(jnp.where(inside, part, -3e38), axis=1, keepdims=True)
                peaks.append(peak)
                wide = jnp.broadcast_to(peak, part.shape) if i == 0 else jnp.where(inside, peak, wide)
            term = jnp.exp2((part - wide) * scale)
            if seen is not None:
                term = jnp.where(seen > 0.5, term, 0.0)
            terms.append(term.astype(BF16))
        outs.append(dot(jnp.concatenate(terms, axis=1), by_head(v, masks, group, True)))
    first, second = outs
    left = lane < LANES // 2
    middle = jnp.where(left, first[:, LANES:], second[:, :LANES])
    den = jnp.where(left, second[:, :LANES], first[:, LANES:])
    den = den + pltpu.roll(den, LANES // 2, 1)
    return jnp.concatenate([first[:, :LANES], middle, second[:, LANES:]], axis=1), peaks, den


def divide(sums, denominator, spreader):
    inverse = 1.0 / denominator
    high = inverse.astype(BF16).astype(F32)
    lane = iota(inverse.shape, 1)
    split = jnp.where(lane < HEADS, high, inverse - high).astype(BF16)
    return (sums * dot(split, spreader)).astype(BF16)


def put(ref, rows, values):
    for j in range(ref.shape[0]):
        ref[j, rows, :] = values[:, j * LANES : (j + 1) * LANES]


def take(ref, rows):
    return jnp.concatenate([ref[j, rows, :] for j in range(ref.shape[0])], axis=1)


def kernel(
    sizes,
    tokens_hbm, visible_ref, virtual_hbm, *rest,
):
    trk_n, frm_n, tracks, frames, virt, width = sizes
    weights_hbm = rest[:10]
    tracks_out, virtual_out = rest[10:12]
    weights = rest[12:22]
    (
        turned, qkv, sums, dens, back_in, updated, pair, virt_rows, virt_query, seen_all,
        send_sum, send_stat, got_sum, got_stat, mine, gathered, back_query, virt_flat,
        virtual_ref, x_sem, w_sem, a_send, a_recv, b_send, b_recv, s_send, s_recv, t_send, t_recv, g_send, g_recv, p_send,
    ) = rest[22:]
    time_qkv, time_out, virt_q, virt_kv, virt_out, self_qkv, self_out, back_q, back_kv, back_out = weights
    scale = (width // HEADS) ** (-0.5) * math.log2(math.e)
    me_t = lax.axis_index("trk")
    me_f = lax.axis_index("frm")
    share = tracks // frm_n
    block = share * frames
    span = frm_n * frames
    always = trk_n == frames

    loads = [
        pltpu.make_async_copy(weights_hbm[j], weights[j], w_sem.at[j]) for j in range(10)
    ]
    load_virtual = pltpu.make_async_copy(virtual_hbm, virtual_ref, x_sem.at[0])
    load_virtual.start()
    for j in (2, 0, 1, 3, 7, 4, 5, 6, 8, 9):
        loads[j].start()

    barrier = pltpu.get_barrier_semaphore()
    for k in range(1, frm_n):
        pl.semaphore_signal(
            barrier, inc=1, device_id=(me_t, lax.rem(me_f + k, frm_n)), device_id_type=MESH
        )
    for k in range(1, trk_n):
        pl.semaphore_signal(
            barrier, inc=1, device_id=(lax.rem(me_t + k, trk_n), me_f), device_id_type=MESH
        )

    mask = head_masks(max(virt, tracks, span), width)
    spread2 = spread(width, 2 * HEADS)

    pl.semaphore_wait(barrier, frm_n + trk_n - 2)

    def rows(index):
        return pl.ds(pl.multiple_of(index * block, block), block)

    def a_copy(k, peer, source):
        return pltpu.make_async_remote_copy(
            src_ref=tokens_hbm.at[rows(peer)],
            dst_ref=turned.at[rows(source)],
            send_sem=a_send.at[peer],
            recv_sem=a_recv.at[source],
            device_id=(me_t, peer),
            device_id_type=MESH,
        )

    def b_copy(peer, source):
        return pltpu.make_async_remote_copy(
            src_ref=back_in.at[rows(peer)],
            dst_ref=updated.at[rows(source)],
            send_sem=b_send.at[peer],
            recv_sem=b_recv.at[source],
            device_id=(me_t, peer),
            device_id_type=MESH,
        )

    own_tokens = pltpu.make_async_copy(
        tokens_hbm.at[rows(me_f)], turned.at[rows(me_f)], x_sem.at[1]
    )
    for k in range(1, frm_n):
        a_copy(k, lax.rem(me_f + k, frm_n), me_f).start()
    own_tokens.start()

    loads[2].wait()
    every = slice(None)
    load_virtual.wait()
    virtual = virtual_ref[...].astype(F32)
    put(virt_rows, every, virtual)
    put(virt_query, every, dot(normalize(virtual), virt_q[...]))
    repeat = jnp.where(
        iota((tracks, LANES), 0) == lax.rem(iota((tracks, LANES), 1), tracks),
        1.0,
        0.0,
    ).astype(BF16)
    seen_all[...] = dot(visible_ref[...].astype(F32).astype(BF16), repeat)
    loads[0].wait()
    own_tokens.wait()
    for k in range(1, frm_n):
        peer = lax.rem(me_f + frm_n - k, frm_n)
        a_copy(k, peer, peer).wait_recv()

    qkv[...] = dot(normalize(turned[...].astype(F32)), time_qkv[...]).reshape(
        frm_n, share, frames, 3 * width
    )
    for n in range(share):
        track = qkv[:, n].reshape(span, 3 * width)
        total, _, den = attend(
            track[:, :width].astype(BF16), track[:, width : 2 * width], track[:, 2 * width :],
            mask, scale,
        )
        sums[:, n] = total.reshape(frm_n, frames, width)
        dens[:, n] = den.reshape(frm_n, frames, LANES)
    all_rows = tracks * frames
    mixed = divide(
        sums[...].reshape(all_rows, width), dens[...].reshape(all_rows, LANES), spread2
    )
    loads[1].wait()
    back_in[...] = (turned[...].astype(F32) + dot(mixed, time_out[...])).astype(BF16)
    for k in range(1, frm_n):
        b_copy(lax.rem(me_f + k, frm_n), me_f).start()
    updated[rows(me_f), :] = back_in[rows(me_f), :]
    loads[3].wait()
    loads[7].wait()
    for k in range(1, frm_n):
        peer = lax.rem(me_f + frm_n - k, frm_n)
        b_copy(peer, peer).wait_recv()

    fresh = normalize(updated[...].astype(F32))
    put(pair, every, dot(fresh, virt_kv[...]))
    pack = jnp.where(
        iota((HEADS, LANES), 0) == ((iota((HEADS, LANES), 1) // HEADS) & (HEADS - 1)), 1.0, 0.0
    ).astype(F32)
    groups = virt // HEADS

    def s_copies(frame, source):
        return (
            pltpu.make_async_remote_copy(
                src_ref=send_sum.at[frame], dst_ref=got_sum.at[source],
                send_sem=s_send.at[frame], recv_sem=s_recv.at[source],
                device_id=(frame, me_f), device_id_type=MESH,
            ),
            pltpu.make_async_remote_copy(
                src_ref=send_stat.at[frame], dst_ref=got_stat.at[source],
                send_sem=t_send.at[frame], recv_sem=t_recv.at[source],
                device_id=(frame, me_f), device_id_type=MESH,
            ),
        )

    def remote(frame, step, act):
        if always:
            if step < frames - 1:
                act()
        else:
            pl.when(frame != me_t)(act)

    def send_partial(frame):
        for copy in s_copies(frame, me_t):
            copy.start()

    for step in range(frames):
        frame = lax.rem(me_t + 1 + step, frames)
        both = take(pair, pl.ds(frame, tracks, stride=frames))
        total, peaks, den = attend(
            take(virt_query, pl.ds(frame, virt, stride=frames)).astype(BF16),
            both[:, :width], both[:, width:],
            mask, scale, seen=seen_all[pl.ds(frame, 1), :],
        )
        send_sum[frame] = total.astype(BF16)
        head = iota((virt, LANES), 1) & (HEADS - 1)
        peak = functools.reduce(
            lambda wide, h: jnp.where(head == h, peaks[h], wide), range(HEADS), jnp.zeros_like(den)
        )
        for j, stat in enumerate((peak, den)):
            send_stat[frame, j] = jnp.sum(stat.reshape(groups, HEADS, LANES) * pack[None], axis=1)
        remote(frame, step, functools.partial(send_partial, frame))

    put(back_query, every, dot(fresh, back_q[...]))
    loads[4].wait()
    loads[5].wait()
    loads[6].wait()

    side = lax.rem(me_t, 2)
    partner = me_t + 1 - 2 * side

    def g_copy(peer, frame):
        return pltpu.make_async_remote_copy(
            src_ref=mine, dst_ref=gathered.at[frame],
            send_sem=g_send.at[peer], recv_sem=g_recv.at[frame],
            device_id=(peer, me_f), device_id_type=MESH,
        )

    def p_copy(frame):
        return pltpu.make_async_remote_copy(
            src_ref=gathered.at[frame], dst_ref=gathered.at[frame],
            send_sem=p_send.at[frame], recv_sem=g_recv.at[frame],
            device_id=(partner, me_f), device_id_type=MESH,
        )

    def own_or(frame, step, own, other):
        if always:
            own() if step == 0 else other()
        else:
            pl.when(frame == me_t)(own)
            pl.when(frame != me_t)(other)

    def own_frame():
        got_sum[me_t] = send_sum[me_t]
        got_stat[me_t] = send_stat[me_t]
        for k in range(1, trk_n):
            peer = lax.rem(me_t + trk_n - k, trk_n)
            for copy in s_copies(me_t, peer):
                copy.wait_recv()
        peaks = got_stat[:, 0]
        factor = jnp.exp2((peaks - jnp.max(peaks, 0, keepdims=True)) * scale)
        factor = factor / jnp.sum(factor * got_stat[:, 1], 0, keepdims=True)
        spread1 = spread(width, HEADS * HEADS)
        attended = jnp.zeros((virt, width), F32)
        for d in range(trk_n):
            wide = (factor[d][:, None, :] * pack[None]).reshape(virt, LANES).astype(BF16)
            attended += got_sum[d].astype(F32) * dot(wide, spread1)
        rows_here = take(virt_rows, pl.ds(me_t, virt, stride=frames))
        cross = (rows_here + dot(attended.astype(BF16), virt_out[...])).astype(BF16).astype(F32)
        proj = dot(normalize(cross), self_qkv[...])
        total, _, den = attend(
            proj[:, :width].astype(BF16), proj[:, width : 2 * width], proj[:, 2 * width :],
            mask, scale,
        )
        self_mixed = divide(total, den, spread2)
        mine[...] = (cross + dot(self_mixed, self_out[...])).astype(BF16)
        for k in range(2, trk_n, 2):
            g_copy(lax.rem(me_t + k, trk_n), me_t).start()
        gathered[me_t] = mine[...]

    if always:
        own_frame()
    else:
        pl.when(me_t < frames)(own_frame)

    loads[8].wait()
    loads[9].wait()
    dens_flat, sums_flat = virt_flat
    for step in range(frames):
        if step < frames // 2:
            frame = lax.rem(me_t + frames - 2 * step, frames)

            def arrived(frame=frame):
                g_copy(frame, frame).wait_recv()

            own_or(frame, step, lambda: None, arrived)
            p_copy(frame).start()
        else:
            frame = lax.rem(partner + frames - 2 * (step - frames // 2), frames)
            p_copy(frame).wait_recv()
        rows_f = gathered[frame].astype(F32)
        put(virt_rows, pl.ds(frame, virt, stride=frames), rows_f)
        back = dot(normalize(rows_f), back_kv[...])
        total, _, den = attend(
            take(back_query, pl.ds(frame, tracks, stride=frames)).astype(BF16),
            back[:, :width], back[:, width:], mask, scale,
        )
        put(sums_flat, pl.ds(frame, tracks, stride=frames), total)
        dens_flat[pl.ds(frame, tracks, stride=frames), :] = den
    back_mixed = divide(take(sums_flat, every), dens_flat[...], spread2)
    tracks_out[...] = (updated[...].astype(F32) + dot(back_mixed, back_out[...])).astype(BF16)
    virtual_out[...] = take(virt_rows, every).astype(BF16)

    for k in range(1, frm_n):
        peer = lax.rem(me_f + k, frm_n)
        a_copy(k, peer, me_f).wait_send()
        b_copy(peer, me_f).wait_send()
    for step in range(frames):
        frame = lax.rem(me_t + 1 + step, frames)

        def left(frame=frame):
            for copy in s_copies(frame, me_t):
                copy.wait_send()

        remote(frame, step, left)

    for step in range(frames // 2):
        p_copy(lax.rem(me_t + 2 * step, frames)).wait_send()

    def own_left():
        for k in range(2, trk_n, 2):
            g_copy(lax.rem(me_t + k, trk_n), me_t).wait_send()

    if always:
        own_left()
    else:
        pl.when(me_t < frames)(own_left)


def on_device(mesh_sizes, tokens, visible, virtual, *weights):
    trk_n, frm_n = mesh_sizes
    tracks, frames, width = tokens.shape
    virt = virtual.shape[0]
    assert trk_n >= frames and trk_n % 2 == 0 and frames % 2 == 0 and tracks % frm_n == 0
    assert width == 3 * LANES and HEADS == 8
    share, span = tracks // frm_n, frm_n * frames
    all_rows, virt_all = tracks * frames, virt * frames
    dma = pltpu.SemaphoreType.DMA
    vmem = pl.BlockSpec(memory_space=pltpu.VMEM)
    hbm = pl.BlockSpec(memory_space=pltpu.HBM)
    scratch = [pltpu.VMEM(w.shape, BF16) for w in weights] + [
        pltpu.VMEM((all_rows, width), BF16),
        pltpu.VMEM((frm_n, share, frames, 3 * width), F32),
        pltpu.VMEM((frm_n, share, frames, width), F32),
        pltpu.VMEM((frm_n, share, frames, LANES), F32),
        pltpu.VMEM((all_rows, width), BF16),
        pltpu.VMEM((all_rows, width), BF16),
        pltpu.VMEM((2 * width // LANES, all_rows, LANES), F32),
        pltpu.VMEM((width // LANES, virt_all, LANES), F32),
        pltpu.VMEM((width // LANES, virt_all, LANES), F32),
        pltpu.VMEM((frames, LANES), F32),
        pltpu.VMEM((frames, virt, width), BF16),
        pltpu.VMEM((frames, 2, virt // HEADS, LANES), F32),
        pltpu.VMEM((trk_n, virt, width), BF16),
        pltpu.VMEM((trk_n, 2, virt // HEADS, LANES), F32),
        pltpu.VMEM((virt, width), BF16),
        pltpu.VMEM((frames, virt, width), BF16),
        pltpu.VMEM((width // LANES, all_rows, LANES), F32),
        [pltpu.VMEM((all_rows, LANES), F32), pltpu.VMEM((width // LANES, all_rows, LANES), F32)],
        pltpu.VMEM((virt_all, width), BF16),
        dma((2,)),
        dma((10,)),
        dma((frm_n,)), dma((frm_n,)), dma((frm_n,)), dma((frm_n,)),
        dma((frames,)), dma((trk_n,)), dma((frames,)), dma((trk_n,)),
        dma((trk_n,)), dma((frames,)), dma((frames,)),
    ]
    tracks_out, virtual_out = pl.pallas_call(
        functools.partial(kernel, (trk_n, frm_n, tracks, frames, virt, width)),
        out_shape=(
            jax.ShapeDtypeStruct((all_rows, width), BF16),
            jax.ShapeDtypeStruct((virt_all, width), BF16),
        ),
        in_specs=[hbm, vmem, hbm] + [hbm] * 10,
        out_specs=(vmem, vmem),
        scratch_shapes=scratch,
        compiler_params=pltpu.CompilerParams(
            collective_id=0, has_side_effects=True, vmem_limit_bytes=64 * 1024 * 1024
        ),
    )(
        tokens.reshape(all_rows, width), jnp.transpose(visible), virtual.reshape(virt_all, width), *weights
    )
    return tracks_out.reshape(tokens.shape), virtual_out.reshape(virtual.shape)


def solution(mesh):
    placed = (P("trk", "frm", None), P("trk", "frm"), P(None, "frm", None)) + (P(),) * 10
    return jax.shard_map(
        functools.partial(on_device, (mesh.shape["trk"], mesh.shape["frm"])),
        mesh=mesh,
        in_specs=placed,
        out_specs=(P("trk", "frm", None), P(None, "frm", None)),
        check_vma=False,
    )
```

```python
import functools
import math

import jax
import jax.numpy as jnp
from jax import lax
from jax.experimental import pallas as pl
from jax.experimental.pallas import tpu as pltpu
from jax.sharding import PartitionSpec as P

HEADS = 8
HALF = HEADS // 2
EPS = 1e-05
NEG = -1e30
LANES = 128
BF16 = jnp.bfloat16
F32 = jnp.float32
MESH = pl.DeviceIdType.MESH


def normalize(values):
    center = jnp.mean(values, -1, keepdims=True)
    shifted = values - center
    return (shifted * lax.rsqrt(jnp.mean(shifted * shifted, -1, keepdims=True) + EPS)).astype(BF16)


def dot(a, b):
    return jnp.dot(a, b, preferred_element_type=F32)


def dot_t(a, b):
    return lax.dot_general(a, b, (((1,), (1,)), ((), ())), preferred_element_type=F32)


def iota(shape, dim):
    return lax.broadcasted_iota(jnp.int32, shape, dim)


def head_masks(rows, width):
    size = width // HEADS
    lane = iota((rows, LANES), 1)
    masks = []
    for h in range(HEADS):
        low, row = h * size, []
        for j in range(width // LANES):
            first, last = low - j * LANES, low + size - j * LANES
            if last <= 0 or first >= LANES:
                row.append(None)
            else:
                row.append(jnp.where((lane >= first) & (lane < last), 1.0, 0.0).astype(BF16))
        masks.append(row)
    return masks


def spread(width, lanes_used):
    size = width // HEADS
    row = iota((LANES, width), 0)
    low = (row & (HEADS - 1)) * size
    lane = iota((LANES, width), 1)
    return jnp.where((row < lanes_used) & (lane >= low) & (lane < low + size), 1.0, 0.0).astype(BF16)


def by_head(x, masks, group, totals=False):
    keys = x.shape[0]
    lane = iota((keys, LANES), 1)
    free = lane >= LANES // 2 if group == 0 else lane < LANES // 2
    copies = []
    for h in range(group * HALF, (group + 1) * HALF):
        tiles = []
        for j in (group, group + 1):
            m = masks[h][j]
            tile = jnp.zeros((keys, LANES), BF16)
            if m is not None:
                tile = x[:, j * LANES : (j + 1) * LANES] * m[:keys]
            if totals and j == 1:
                ones = jnp.where(free & ((lane & (HEADS - 1)) == h), 1.0, 0.0).astype(BF16)
                tile = ones if m is None else tile + ones
            tiles.append(tile)
        copies.append(jnp.concatenate(tiles, axis=1))
    return jnp.concatenate(copies, axis=0)


def attend(items, masks, scale):
    rows, keys = items[0][0].shape[0], items[0][1].shape[0]
    per = LANES // keys
    lane = iota((rows, LANES), 1)
    inside = [(lane >= i * keys) & (lane < (i + 1) * keys) for i in range(per)]
    windows = [slice(group * LANES, (group + 2) * LANES) for group in range(2)]
    scores = [
        [dot_t(q[:, windows[group]], by_head(k.astype(BF16), masks, group)) for group in range(2)]
        for q, k, _, _ in items
    ]
    all_peaks, all_terms = [], []
    for both, (_, _, _, seen) in zip(scores, items):
        peaks, halves = [], []
        for score in both:
            terms = []
            for j in range(HALF * keys // LANES):
                part = score[:, j * LANES : (j + 1) * LANES]
                if seen is not None:
                    part = jnp.where(seen > 0.5, part, NEG)
                wide = None
                for i in range(per):
                    peak = jnp.max(jnp.where(inside[i], part, -3e38), axis=1, keepdims=True)
                    peaks.append(peak)
                    wide = (
                        jnp.broadcast_to(peak, part.shape)
                        if i == 0
                        else jnp.where(inside[i], peak, wide)
                    )
                term = jnp.exp2((part - wide) * scale)
                if seen is not None:
                    term = jnp.where(seen > 0.5, term, 0.0)
                terms.append(term.astype(BF16))
            halves.append(jnp.concatenate(terms, axis=1))
        all_peaks.append(peaks)
        all_terms.append(halves)
    outs = [
        [dot(half, by_head(v.astype(BF16), masks, group, True)) for group, half in enumerate(halves)]
        for halves, (_, _, v, _) in zip(all_terms, items)
    ]
    left = lane < LANES // 2
    results = []
    for (first, second), peaks in zip(outs, all_peaks):
        middle = jnp.where(left, first[:, LANES:], second[:, :LANES])
        den = jnp.where(left, second[:, :LANES], first[:, LANES:])
        den = den + pltpu.roll(den, LANES // 2, 1)
        total = jnp.concatenate([first[:, :LANES], middle, second[:, LANES:]], axis=1)
        results.append((total, peaks, den))
    return results


def divide(sums, denominator, spreader):
    inverse = 1.0 / denominator
    high = inverse.astype(BF16).astype(F32)
    lane = iota(inverse.shape, 1)
    split = jnp.where(lane < HEADS, high, inverse - high).astype(BF16)
    return (sums * dot(split, spreader)).astype(BF16)


def put(ref, rows, values):
    for j in range(ref.shape[0]):
        ref[j, rows, :] = values[:, j * LANES : (j + 1) * LANES]


def take(ref, rows):
    return jnp.concatenate([ref[j, rows, :] for j in range(ref.shape[0])], axis=1)


def kernel(
    sizes,
    tokens_hbm, visible_ref, virtual_hbm, *rest,
):
    trk_n, frm_n, tracks, frames, virt, width = sizes
    weights_hbm = rest[:10]
    tracks_out, virtual_out = rest[10:12]
    weights = rest[12:22]
    (
        turned, qkv, sums, dens, back_in, updated, pair, virt_rows, virt_query, seen_all,
        send_sum, send_stat, got_sum, got_stat, mine, gathered, back_query, virt_flat,
        virtual_ref, x_sem, w_sem, a_send, a_recv, b_send, b_recv, s_send, s_recv, t_send, t_recv, g_send, g_recv, p_send,
    ) = rest[22:]
    time_qkv, time_out, virt_q, virt_kv, virt_out, self_qkv, self_out, back_q, back_kv, back_out = weights
    scale = (width // HEADS) ** (-0.5) * math.log2(math.e)
    me_t = lax.axis_index("trk")
    me_f = lax.axis_index("frm")
    share = tracks // frm_n
    block = share * frames
    span = frm_n * frames
    always = trk_n == frames

    loads = [
        pltpu.make_async_copy(weights_hbm[j], weights[j], w_sem.at[j]) for j in range(10)
    ]
    load_virtual = pltpu.make_async_copy(virtual_hbm, virtual_ref, x_sem.at[0])
    load_virtual.start()
    for j in (2, 0, 1, 3, 7, 4, 5, 6, 8, 9):
        loads[j].start()

    barrier = pltpu.get_barrier_semaphore()
    for k in range(1, frm_n):
        pl.semaphore_signal(
            barrier, inc=1, device_id=(me_t, lax.rem(me_f + k, frm_n)), device_id_type=MESH
        )
    for k in range(1, trk_n):
        pl.semaphore_signal(
            barrier, inc=1, device_id=(lax.rem(me_t + k, trk_n), me_f), device_id_type=MESH
        )

    mask = head_masks(max(virt, tracks, span), width)
    spread2 = spread(width, 2 * HEADS)

    pl.semaphore_wait(barrier, frm_n + trk_n - 2)

    def rows(index):
        return pl.ds(pl.multiple_of(index * block, block), block)

    def a_copy(k, peer, source):
        return pltpu.make_async_remote_copy(
            src_ref=tokens_hbm.at[rows(peer)],
            dst_ref=turned.at[rows(source)],
            send_sem=a_send.at[peer],
            recv_sem=a_recv.at[source],
            device_id=(me_t, peer),
            device_id_type=MESH,
        )

    def b_copy(peer, source):
        return pltpu.make_async_remote_copy(
            src_ref=back_in.at[rows(peer)],
            dst_ref=updated.at[rows(source)],
            send_sem=b_send.at[peer],
            recv_sem=b_recv.at[source],
            device_id=(me_t, peer),
            device_id_type=MESH,
        )

    own_tokens = pltpu.make_async_copy(
        tokens_hbm.at[rows(me_f)], turned.at[rows(me_f)], x_sem.at[1]
    )
    for k in range(1, frm_n):
        a_copy(k, lax.rem(me_f + k, frm_n), me_f).start()
    own_tokens.start()

    loads[2].wait()
    every = slice(None)
    load_virtual.wait()
    virtual = virtual_ref[...].astype(F32)
    put(virt_rows, every, virtual)
    put(virt_query, every, dot(normalize(virtual), virt_q[...]))
    repeat = jnp.where(
        iota((tracks, LANES), 0) == lax.rem(iota((tracks, LANES), 1), tracks),
        1.0,
        0.0,
    ).astype(BF16)
    seen_all[...] = dot(visible_ref[...].astype(F32).astype(BF16), repeat)
    loads[0].wait()
    own_tokens.wait()
    for k in range(1, frm_n):
        peer = lax.rem(me_f + frm_n - k, frm_n)
        a_copy(k, peer, peer).wait_recv()

    qkv[...] = dot(normalize(turned[...].astype(F32)), time_qkv[...]).reshape(
        frm_n, share, frames, 3 * width
    )
    items = []
    for n in range(share):
        track = qkv[:, n].reshape(span, 3 * width)
        items.append(
            (track[:, :width].astype(BF16), track[:, width : 2 * width], track[:, 2 * width :], None)
        )
    for n, (total, _, den) in enumerate(attend(items, mask, scale)):
        sums[:, n] = total.reshape(frm_n, frames, width)
        dens[:, n] = den.reshape(frm_n, frames, LANES)
    all_rows = tracks * frames
    mixed = divide(
        sums[...].reshape(all_rows, width), dens[...].reshape(all_rows, LANES), spread2
    )
    loads[1].wait()
    back_in[...] = (turned[...].astype(F32) + dot(mixed, time_out[...])).astype(BF16)
    for k in range(1, frm_n):
        b_copy(lax.rem(me_f + k, frm_n), me_f).start()
    updated[rows(me_f), :] = back_in[rows(me_f), :]
    loads[3].wait()
    loads[7].wait()
    for k in range(1, frm_n):
        peer = lax.rem(me_f + frm_n - k, frm_n)
        b_copy(peer, peer).wait_recv()

    fresh = normalize(updated[...].astype(F32))
    put(pair, every, dot(fresh, virt_kv[...]))
    pack = jnp.where(
        iota((HEADS, LANES), 0) == ((iota((HEADS, LANES), 1) // HEADS) & (HEADS - 1)), 1.0, 0.0
    ).astype(F32)
    groups = virt // HEADS

    def s_copies(frame, source):
        return (
            pltpu.make_async_remote_copy(
                src_ref=send_sum.at[frame], dst_ref=got_sum.at[source],
                send_sem=s_send.at[frame], recv_sem=s_recv.at[source],
                device_id=(frame, me_f), device_id_type=MESH,
            ),
            pltpu.make_async_remote_copy(
                src_ref=send_stat.at[frame], dst_ref=got_stat.at[source],
                send_sem=t_send.at[frame], recv_sem=t_recv.at[source],
                device_id=(frame, me_f), device_id_type=MESH,
            ),
        )

    def remote(frame, step, act):
        if always:
            if step < frames - 1:
                act()
        else:
            pl.when(frame != me_t)(act)

    def send_partial(frame):
        for copy in s_copies(frame, me_t):
            copy.start()

    head = iota((virt, LANES), 1) & (HEADS - 1)
    batch = frames // 2
    for start in range(0, frames, batch):
        steps = range(start, start + batch)
        order = [lax.rem(me_t + 1 + step, frames) for step in steps]
        items = []
        for frame in order:
            both = take(pair, pl.ds(frame, tracks, stride=frames))
            query = take(virt_query, pl.ds(frame, virt, stride=frames)).astype(BF16)
            items.append((query, both[:, :width], both[:, width:], seen_all[pl.ds(frame, 1), :]))
        for step, frame, (total, peaks, den) in zip(steps, order, attend(items, mask, scale)):
            send_sum[frame] = total.astype(BF16)
            peak = functools.reduce(
                lambda wide, h: jnp.where(head == h, peaks[h], wide), range(HEADS), jnp.zeros_like(den)
            )
            for j, stat in enumerate((peak, den)):
                send_stat[frame, j] = jnp.sum(
                    stat.reshape(groups, HEADS, LANES) * pack[None], axis=1
                )
        for step, frame in zip(steps, order):
            remote(frame, step, functools.partial(send_partial, frame))

    put(back_query, every, dot(fresh, back_q[...]))
    loads[4].wait()
    loads[5].wait()
    loads[6].wait()

    side = lax.rem(me_t, 2)
    partner = me_t + 1 - 2 * side

    def g_copy(peer, frame):
        return pltpu.make_async_remote_copy(
            src_ref=mine, dst_ref=gathered.at[frame],
            send_sem=g_send.at[peer], recv_sem=g_recv.at[frame],
            device_id=(peer, me_f), device_id_type=MESH,
        )

    def p_copy(frame):
        return pltpu.make_async_remote_copy(
            src_ref=gathered.at[frame], dst_ref=gathered.at[frame],
            send_sem=p_send.at[frame], recv_sem=g_recv.at[frame],
            device_id=(partner, me_f), device_id_type=MESH,
        )

    def own_or(frame, step, own, other):
        if always:
            own() if step == 0 else other()
        else:
            pl.when(frame == me_t)(own)
            pl.when(frame != me_t)(other)

    def own_frame():
        got_sum[me_t] = send_sum[me_t]
        got_stat[me_t] = send_stat[me_t]
        for k in range(1, trk_n):
            peer = lax.rem(me_t + trk_n - k, trk_n)
            for copy in s_copies(me_t, peer):
                copy.wait_recv()
        peaks = got_stat[:, 0]
        factor = jnp.exp2((peaks - jnp.max(peaks, 0, keepdims=True)) * scale)
        factor = factor / jnp.sum(factor * got_stat[:, 1], 0, keepdims=True)
        spread1 = spread(width, HEADS * HEADS)
        attended = jnp.zeros((virt, width), F32)
        for d in range(trk_n):
            wide = (factor[d][:, None, :] * pack[None]).reshape(virt, LANES).astype(BF16)
            attended += got_sum[d].astype(F32) * dot(wide, spread1)
        rows_here = take(virt_rows, pl.ds(me_t, virt, stride=frames))
        cross = (rows_here + dot(attended.astype(BF16), virt_out[...])).astype(BF16).astype(F32)
        proj = dot(normalize(cross), self_qkv[...])
        item = (proj[:, :width].astype(BF16), proj[:, width : 2 * width], proj[:, 2 * width :], None)
        total, _, den = attend([item], mask, scale)[0]
        self_mixed = divide(total, den, spread2)
        mine[...] = (cross + dot(self_mixed, self_out[...])).astype(BF16)
        for k in range(2, trk_n, 2):
            g_copy(lax.rem(me_t + k, trk_n), me_t).start()
        gathered[me_t] = mine[...]

    if always:
        own_frame()
    else:
        pl.when(me_t < frames)(own_frame)

    loads[8].wait()
    loads[9].wait()
    dens_flat, sums_flat = virt_flat

    def back(order):
        rows_f = [gathered[frame].astype(F32) for frame in order]
        for frame, values in zip(order, rows_f):
            put(virt_rows, pl.ds(frame, virt, stride=frames), values)
        both = dot(normalize(jnp.concatenate(rows_f, axis=0)), back_kv[...])
        items = []
        for j, frame in enumerate(order):
            query = take(back_query, pl.ds(frame, tracks, stride=frames)).astype(BF16)
            part = both[j * virt : (j + 1) * virt]
            items.append((query, part[:, :width], part[:, width:], None))
        for frame, (total, _, den) in zip(order, attend(items, mask, scale)):
            put(sums_flat, pl.ds(frame, tracks, stride=frames), total)
            dens_flat[pl.ds(frame, tracks, stride=frames), :] = den

    mine_first = [lax.rem(me_t + frames - 2 * step, frames) for step in range(frames // 2)]
    for step, frame in enumerate(mine_first):

        def arrived(frame=frame):
            g_copy(frame, frame).wait_recv()

        own_or(frame, step, lambda: None, arrived)
        p_copy(frame).start()
        if step == 0:
            back([frame])
    back(mine_first[1:])
    others = [lax.rem(partner + frames - 2 * step, frames) for step in range(frames // 2)]
    for frame in others:
        p_copy(frame).wait_recv()
    back(others)
    back_mixed = divide(take(sums_flat, every), dens_flat[...], spread2)
    tracks_out[...] = (updated[...].astype(F32) + dot(back_mixed, back_out[...])).astype(BF16)
    virtual_out[...] = take(virt_rows, every).astype(BF16)

    for k in range(1, frm_n):
        peer = lax.rem(me_f + k, frm_n)
        a_copy(k, peer, me_f).wait_send()
        b_copy(peer, me_f).wait_send()
    for step in range(frames):
        frame = lax.rem(me_t + 1 + step, frames)

        def left(frame=frame):
            for copy in s_copies(frame, me_t):
                copy.wait_send()

        remote(frame, step, left)

    for step in range(frames // 2):
        p_copy(lax.rem(me_t + 2 * step, frames)).wait_send()

    def own_left():
        for k in range(2, trk_n, 2):
            g_copy(lax.rem(me_t + k, trk_n), me_t).wait_send()

    if always:
        own_left()
    else:
        pl.when(me_t < frames)(own_left)


def on_device(mesh_sizes, tokens, visible, virtual, *weights):
    trk_n, frm_n = mesh_sizes
    tracks, frames, width = tokens.shape
    virt = virtual.shape[0]
    assert trk_n >= frames and trk_n % 2 == 0 and frames % 2 == 0 and tracks % frm_n == 0
    assert width == 3 * LANES and HEADS == 8
    share, span = tracks // frm_n, frm_n * frames
    all_rows, virt_all = tracks * frames, virt * frames
    dma = pltpu.SemaphoreType.DMA
    vmem = pl.BlockSpec(memory_space=pltpu.VMEM)
    hbm = pl.BlockSpec(memory_space=pltpu.HBM)
    scratch = [pltpu.VMEM(w.shape, BF16) for w in weights] + [
        pltpu.VMEM((all_rows, width), BF16),
        pltpu.VMEM((frm_n, share, frames, 3 * width), F32),
        pltpu.VMEM((frm_n, share, frames, width), F32),
        pltpu.VMEM((frm_n, share, frames, LANES), F32),
        pltpu.VMEM((all_rows, width), BF16),
        pltpu.VMEM((all_rows, width), BF16),
        pltpu.VMEM((2 * width // LANES, all_rows, LANES), F32),
        pltpu.VMEM((width // LANES, virt_all, LANES), F32),
        pltpu.VMEM((width // LANES, virt_all, LANES), F32),
        pltpu.VMEM((frames, LANES), F32),
        pltpu.VMEM((frames, virt, width), BF16),
        pltpu.VMEM((frames, 2, virt // HEADS, LANES), F32),
        pltpu.VMEM((trk_n, virt, width), BF16),
        pltpu.VMEM((trk_n, 2, virt // HEADS, LANES), F32),
        pltpu.VMEM((virt, width), BF16),
        pltpu.VMEM((frames, virt, width), BF16),
        pltpu.VMEM((width // LANES, all_rows, LANES), F32),
        [pltpu.VMEM((all_rows, LANES), F32), pltpu.VMEM((width // LANES, all_rows, LANES), F32)],
        pltpu.VMEM((virt_all, width), BF16),
        dma((2,)),
        dma((10,)),
        dma((frm_n,)), dma((frm_n,)), dma((frm_n,)), dma((frm_n,)),
        dma((frames,)), dma((trk_n,)), dma((frames,)), dma((trk_n,)),
        dma((trk_n,)), dma((frames,)), dma((frames,)),
    ]
    tracks_out, virtual_out = pl.pallas_call(
        functools.partial(kernel, (trk_n, frm_n, tracks, frames, virt, width)),
        out_shape=(
            jax.ShapeDtypeStruct((all_rows, width), BF16),
            jax.ShapeDtypeStruct((virt_all, width), BF16),
        ),
        in_specs=[hbm, vmem, hbm] + [hbm] * 10,
        out_specs=(vmem, vmem),
        scratch_shapes=scratch,
        compiler_params=pltpu.CompilerParams(
            collective_id=0, has_side_effects=True, vmem_limit_bytes=64 * 1024 * 1024
        ),
    )(
        tokens.reshape(all_rows, width), jnp.transpose(visible), virtual.reshape(virt_all, width), *weights
    )
    return tracks_out.reshape(tokens.shape), virtual_out.reshape(virtual.shape)


def solution(mesh):
    placed = (P("trk", "frm", None), P("trk", "frm"), P(None, "frm", None)) + (P(),) * 10
    return jax.shard_map(
        functools.partial(on_device, (mesh.shape["trk"], mesh.shape["frm"])),
        mesh=mesh,
        in_specs=placed,
        out_specs=(P("trk", "frm", None), P(None, "frm", None)),
        check_vma=False,
    )
```

```python
import functools
import math

import jax
import jax.numpy as jnp
from jax import lax
from jax.experimental import pallas as pl
from jax.experimental.pallas import tpu as pltpu
from jax.sharding import PartitionSpec as P

HEADS = 8
HALF = HEADS // 2
EPS = 1e-05
NEG = -1e30
LANES = 128
BF16 = jnp.bfloat16
F32 = jnp.float32
MESH = pl.DeviceIdType.MESH


def normalize(values):
    center = jnp.mean(values, -1, keepdims=True)
    shifted = values - center
    return (shifted * lax.rsqrt(jnp.mean(shifted * shifted, -1, keepdims=True) + EPS)).astype(BF16)


def dot(a, b):
    return jnp.dot(a, b, preferred_element_type=F32)


def dot_t(a, b):
    return lax.dot_general(a, b, (((1,), (1,)), ((), ())), preferred_element_type=F32)


def iota(shape, dim):
    return lax.broadcasted_iota(jnp.int32, shape, dim)


def head_masks(rows, width):
    size = width // HEADS
    lane = iota((rows, LANES), 1)
    masks = []
    for h in range(HEADS):
        low, row = h * size, []
        for j in range(width // LANES):
            first, last = low - j * LANES, low + size - j * LANES
            if last <= 0 or first >= LANES:
                row.append(None)
            else:
                row.append(jnp.where((lane >= first) & (lane < last), 1.0, 0.0).astype(BF16))
        masks.append(row)
    return masks


def spread(width, lanes_used):
    size = width // HEADS
    row = iota((LANES, width), 0)
    low = (row & (HEADS - 1)) * size
    lane = iota((LANES, width), 1)
    return jnp.where((row < lanes_used) & (lane >= low) & (lane < low + size), 1.0, 0.0).astype(BF16)


def by_head(x, masks, group, totals=False):
    keys = x.shape[0]
    lane = iota((keys, LANES), 1)
    free = lane >= LANES // 2 if group == 0 else lane < LANES // 2
    copies = []
    for h in range(group * HALF, (group + 1) * HALF):
        tiles = []
        for j in (group, group + 1):
            m = masks[h][j]
            tile = jnp.zeros((keys, LANES), BF16)
            if m is not None:
                tile = x[:, j * LANES : (j + 1) * LANES] * m[:keys]
            if totals and j == 1:
                ones = jnp.where(free & ((lane & (HEADS - 1)) == h), 1.0, 0.0).astype(BF16)
                tile = ones if m is None else tile + ones
            tiles.append(tile)
        copies.append(jnp.concatenate(tiles, axis=1))
    return jnp.concatenate(copies, axis=0)


def attend(items, masks, scale):
    rows, keys = items[0][0].shape[0], items[0][1].shape[0]
    per = LANES // keys
    lane = iota((rows, LANES), 1)
    inside = [(lane >= i * keys) & (lane < (i + 1) * keys) for i in range(per)]
    windows = [slice(group * LANES, (group + 2) * LANES) for group in range(2)]
    scores = [
        [dot_t(q[:, windows[group]], by_head(k.astype(BF16), masks, group)) for group in range(2)]
        for q, k, _, _ in items
    ]
    all_peaks, all_terms = [], []
    for both, (_, _, _, seen) in zip(scores, items):
        peaks, halves = [], []
        for score in both:
            terms = []
            for j in range(HALF * keys // LANES):
                part = score[:, j * LANES : (j + 1) * LANES]
                if seen is not None:
                    part = jnp.where(seen > 0.5, part, NEG)
                wide = None
                for i in range(per):
                    peak = jnp.max(jnp.where(inside[i], part, -3e38), axis=1, keepdims=True)
                    peaks.append(peak)
                    wide = (
                        jnp.broadcast_to(peak, part.shape)
                        if i == 0
                        else jnp.where(inside[i], peak, wide)
                    )
                term = jnp.exp2((part - wide) * scale)
                if seen is not None:
                    term = jnp.where(seen > 0.5, term, 0.0)
                terms.append(term.astype(BF16))
            halves.append(jnp.concatenate(terms, axis=1))
        all_peaks.append(peaks)
        all_terms.append(halves)
    outs = [
        [dot(half, by_head(v.astype(BF16), masks, group, True)) for group, half in enumerate(halves)]
        for halves, (_, _, v, _) in zip(all_terms, items)
    ]
    left = lane < LANES // 2
    results = []
    for (first, second), peaks in zip(outs, all_peaks):
        middle = jnp.where(left, first[:, LANES:], second[:, :LANES])
        den = jnp.where(left, second[:, :LANES], first[:, LANES:])
        den = den + pltpu.roll(den, LANES // 2, 1)
        total = jnp.concatenate([first[:, :LANES], middle, second[:, LANES:]], axis=1)
        results.append((total, peaks, den))
    return results


def attend_rows(q, k, v, masks, scale, seen=None):
    rows = q.shape[0]
    tiles = [jnp.zeros((rows, LANES), F32) for _ in range(q.shape[1] // LANES)]
    windows = [slice(group * LANES, (group + 2) * LANES) for group in range(2)]
    scores = [dot_t(by_head(q, masks, group), k[:, windows[group]]) for group in range(2)]
    outs, inverses = [], []
    for group, score in enumerate(scores):
        if seen is not None:
            score = jnp.where(seen > 0.5, score, NEG)
        terms = jnp.exp2((score - jnp.max(score, axis=1, keepdims=True)) * scale)
        if seen is not None:
            terms = jnp.where(seen > 0.5, terms, 0.0)
        inverses.append(1.0 / jnp.sum(terms, axis=1, keepdims=True))
        outs.append(dot(terms.astype(BF16), v[:, windows[group]]))
    for group, (out, inverse) in enumerate(zip(outs, inverses)):
        for i in range(HALF):
            part = slice(i * rows, (i + 1) * rows)
            for j in (group, group + 1):
                m = masks[group * HALF + i][j]
                if m is not None:
                    piece = out[part, (j - group) * LANES : (j - group + 1) * LANES]
                    tiles[j] += piece * inverse[part] * m[:rows].astype(F32)
    return jnp.concatenate(tiles, axis=1).astype(BF16)


def divide(sums, denominator, spreader):
    inverse = 1.0 / denominator
    high = inverse.astype(BF16).astype(F32)
    lane = iota(inverse.shape, 1)
    split = jnp.where(lane < HEADS, high, inverse - high).astype(BF16)
    return (sums * dot(split, spreader)).astype(BF16)


def put(ref, rows, values):
    for j in range(ref.shape[0]):
        ref[j, rows, :] = values[:, j * LANES : (j + 1) * LANES]


def take(ref, rows):
    return jnp.concatenate([ref[j, rows, :] for j in range(ref.shape[0])], axis=1)


def kernel(
    sizes,
    tokens_hbm, visible_ref, virtual_hbm, *rest,
):
    trk_n, frm_n, tracks, frames, virt, width = sizes
    weights_hbm = rest[:10]
    tracks_out, virtual_out = rest[10:12]
    weights = rest[12:22]
    (
        turned, qkv, sums, dens, back_in, updated, upd_rows, virt_rows, seen_all,
        send_rows, send_seen, got_rows, got_seen, mine, gathered, back_query, virt_flat,
        virtual_ref, x_sem, w_sem, a_send, a_recv, b_send, b_recv, s_send, s_recv, t_send, t_recv, g_send, g_recv, p_send,
    ) = rest[22:]
    time_qkv, time_out, virt_q, virt_kv, virt_out, self_qkv, self_out, back_q, back_kv, back_out = weights
    scale = (width // HEADS) ** (-0.5) * math.log2(math.e)
    me_t = lax.axis_index("trk")
    me_f = lax.axis_index("frm")
    share = tracks // frm_n
    block = share * frames
    span = frm_n * frames
    always = trk_n == frames

    loads = [
        pltpu.make_async_copy(weights_hbm[j], weights[j], w_sem.at[j]) for j in range(10)
    ]
    load_virtual = pltpu.make_async_copy(virtual_hbm, virtual_ref, x_sem.at[0])
    load_virtual.start()
    for j in (2, 0, 1, 3, 7, 4, 5, 6, 8, 9):
        loads[j].start()

    barrier = pltpu.get_barrier_semaphore()
    for k in range(1, frm_n):
        pl.semaphore_signal(
            barrier, inc=1, device_id=(me_t, lax.rem(me_f + k, frm_n)), device_id_type=MESH
        )
    for k in range(1, trk_n):
        pl.semaphore_signal(
            barrier, inc=1, device_id=(lax.rem(me_t + k, trk_n), me_f), device_id_type=MESH
        )

    mask = head_masks(max(virt, tracks, span), width)
    spread2 = spread(width, 2 * HEADS)

    pl.semaphore_wait(barrier, frm_n + trk_n - 2)

    def rows(index):
        return pl.ds(pl.multiple_of(index * block, block), block)

    def a_copy(k, peer, source):
        return pltpu.make_async_remote_copy(
            src_ref=tokens_hbm.at[rows(peer)],
            dst_ref=turned.at[rows(source)],
            send_sem=a_send.at[peer],
            recv_sem=a_recv.at[source],
            device_id=(me_t, peer),
            device_id_type=MESH,
        )

    def b_copy(peer, source):
        return pltpu.make_async_remote_copy(
            src_ref=back_in.at[rows(peer)],
            dst_ref=updated.at[rows(source)],
            send_sem=b_send.at[peer],
            recv_sem=b_recv.at[source],
            device_id=(me_t, peer),
            device_id_type=MESH,
        )

    def s_copy(frame, source):
        return pltpu.make_async_remote_copy(
            src_ref=send_rows.at[frame], dst_ref=got_rows.at[source],
            send_sem=s_send.at[frame], recv_sem=s_recv.at[source],
            device_id=(frame, me_f), device_id_type=MESH,
        )

    def t_copy(frame, source):
        return pltpu.make_async_remote_copy(
            src_ref=send_seen.at[frame], dst_ref=got_seen.at[source],
            send_sem=t_send.at[frame], recv_sem=t_recv.at[source],
            device_id=(frame, me_f), device_id_type=MESH,
        )

    def remote(frame, step, act):
        if always:
            if step < frames - 1:
                act()
        else:
            pl.when(frame != me_t)(act)

    own_tokens = pltpu.make_async_copy(
        tokens_hbm.at[rows(me_f)], turned.at[rows(me_f)], x_sem.at[1]
    )
    for k in range(1, frm_n):
        a_copy(k, lax.rem(me_f + k, frm_n), me_f).start()
    own_tokens.start()

    loads[2].wait()
    every = slice(None)
    load_virtual.wait()
    virtual = virtual_ref[...].astype(F32)
    put(virt_rows, every, virtual)
    own = lax.rem(me_t, frames)
    rows_here = take(virt_rows, pl.ds(own, virt, stride=frames))
    virt_query = dot(normalize(rows_here), virt_q[...]).astype(BF16)
    repeat = jnp.where(
        iota((tracks, LANES), 0) == lax.rem(iota((tracks, LANES), 1), tracks), 1.0, 0.0
    ).astype(BF16)
    seen_all[...] = dot(visible_ref[...].astype(F32).astype(BF16), repeat)
    for step in range(frames):
        frame = lax.rem(me_t + 1 + step, frames)
        send_seen[frame] = jnp.broadcast_to(seen_all[pl.ds(frame, 1), :], (HEADS, LANES))
        remote(frame, step, lambda: t_copy(frame, me_t).start())
    loads[0].wait()
    own_tokens.wait()
    for k in range(1, frm_n):
        peer = lax.rem(me_f + frm_n - k, frm_n)
        a_copy(k, peer, peer).wait_recv()

    qkv[...] = dot(normalize(turned[...].astype(F32)), time_qkv[...]).reshape(
        frm_n, share, frames, 3 * width
    )
    items = []
    for n in range(share):
        track = qkv[:, n].reshape(span, 3 * width)
        items.append(
            (track[:, :width].astype(BF16), track[:, width : 2 * width], track[:, 2 * width :], None)
        )
    for n, (total, _, den) in enumerate(attend(items, mask, scale)):
        sums[:, n] = total.reshape(frm_n, frames, width)
        dens[:, n] = den.reshape(frm_n, frames, LANES)
    all_rows = tracks * frames
    mixed = divide(
        sums[...].reshape(all_rows, width), dens[...].reshape(all_rows, LANES), spread2
    )
    loads[1].wait()
    back_in[...] = (turned[...].astype(F32) + dot(mixed, time_out[...])).astype(BF16)
    for k in range(1, frm_n):
        b_copy(lax.rem(me_f + k, frm_n), me_f).start()
    updated[rows(me_f), :] = back_in[rows(me_f), :]
    loads[3].wait()
    loads[7].wait()
    for k in range(1, frm_n):
        peer = lax.rem(me_f + frm_n - k, frm_n)
        b_copy(peer, peer).wait_recv()

    now = updated[...].astype(F32)
    put(upd_rows, every, now)
    for step in range(frames):
        frame = lax.rem(me_t + 1 + step, frames)
        send_rows[frame] = take(upd_rows, pl.ds(frame, tracks, stride=frames)).astype(BF16)
        remote(frame, step, lambda: s_copy(frame, me_t).start())
    fresh = normalize(now)
    put(back_query, every, dot(fresh, back_q[...]))
    loads[4].wait()
    loads[5].wait()
    loads[6].wait()

    side = lax.rem(me_t, 2)
    partner = me_t + 1 - 2 * side

    def g_copy(peer, frame):
        return pltpu.make_async_remote_copy(
            src_ref=mine, dst_ref=gathered.at[frame],
            send_sem=g_send.at[peer], recv_sem=g_recv.at[frame],
            device_id=(peer, me_f), device_id_type=MESH,
        )

    def p_copy(frame):
        return pltpu.make_async_remote_copy(
            src_ref=gathered.at[frame], dst_ref=gathered.at[frame],
            send_sem=p_send.at[frame], recv_sem=g_recv.at[frame],
            device_id=(partner, me_f), device_id_type=MESH,
        )

    def own_or(frame, step, own, other):
        if always:
            own() if step == 0 else other()
        else:
            pl.when(frame == me_t)(own)
            pl.when(frame != me_t)(other)

    def own_frame():
        got_rows[me_t] = send_rows[me_t]
        got_seen[me_t] = send_seen[me_t]
        for k in range(1, trk_n):
            peer = lax.rem(me_t + trk_n - k, trk_n)
            t_copy(me_t, peer).wait_recv()
        for k in range(1, trk_n):
            peer = lax.rem(me_t + trk_n - k, trk_n)
            s_copy(me_t, peer).wait_recv()
        lane = iota((1, LANES), 1)
        per = LANES // tracks
        seen = []
        for j in range(0, trk_n, per):
            tile = got_seen[j, :1, :]
            for i in range(1, per):
                tile = jnp.where(lane >= i * tracks, got_seen[j + i, :1, :], tile)
            seen.append(tile)
        seen = jnp.concatenate(seen, axis=1)
        everyone = normalize(got_rows[...].astype(F32).reshape(trk_n * tracks, width))
        pair = dot(everyone, virt_kv[...]).astype(BF16)
        attended = attend_rows(
            virt_query, pair[:, :width], pair[:, width:], mask, scale, seen
        )
        cross = (rows_here + dot(attended, virt_out[...])).astype(BF16).astype(F32)
        proj = dot(normalize(cross), self_qkv[...])
        proj = proj.astype(BF16)
        self_mixed = attend_rows(
            proj[:, :width], proj[:, width : 2 * width], proj[:, 2 * width :], mask, scale
        )
        mine[...] = (cross + dot(self_mixed, self_out[...])).astype(BF16)
        for k in range(2, trk_n, 2):
            g_copy(lax.rem(me_t + k, trk_n), me_t).start()
        gathered[me_t] = mine[...]

    if always:
        own_frame()
    else:
        pl.when(me_t < frames)(own_frame)

    loads[8].wait()
    loads[9].wait()
    dens_flat, sums_flat = virt_flat

    def back(order):
        rows_f = [gathered[frame].astype(F32) for frame in order]
        for frame, values in zip(order, rows_f):
            put(virt_rows, pl.ds(frame, virt, stride=frames), values)
        both = dot(normalize(jnp.concatenate(rows_f, axis=0)), back_kv[...])
        items = []
        for j, frame in enumerate(order):
            query = take(back_query, pl.ds(frame, tracks, stride=frames)).astype(BF16)
            part = both[j * virt : (j + 1) * virt]
            items.append((query, part[:, :width], part[:, width:], None))
        for frame, (total, _, den) in zip(order, attend(items, mask, scale)):
            put(sums_flat, pl.ds(frame, tracks, stride=frames), total)
            dens_flat[pl.ds(frame, tracks, stride=frames), :] = den

    mine_first = [lax.rem(me_t + frames - 2 * step, frames) for step in range(frames // 2)]
    for step, frame in enumerate(mine_first):

        def arrived(frame=frame):
            g_copy(frame, frame).wait_recv()

        own_or(frame, step, lambda: None, arrived)
        p_copy(frame).start()
        if step == 0:
            back([frame])
    back(mine_first[1:])
    others = [lax.rem(partner + frames - 2 * step, frames) for step in range(frames // 2)]
    for frame in others:
        p_copy(frame).wait_recv()
    back(others)
    back_mixed = divide(take(sums_flat, every), dens_flat[...], spread2)
    tracks_out[...] = (updated[...].astype(F32) + dot(back_mixed, back_out[...])).astype(BF16)
    virtual_out[...] = take(virt_rows, every).astype(BF16)

    for k in range(1, frm_n):
        peer = lax.rem(me_f + k, frm_n)
        a_copy(k, peer, me_f).wait_send()
        b_copy(peer, me_f).wait_send()
    for step in range(frames):
        frame = lax.rem(me_t + 1 + step, frames)

        def left(frame=frame):
            s_copy(frame, me_t).wait_send()
            t_copy(frame, me_t).wait_send()

        remote(frame, step, left)

    for step in range(frames // 2):
        p_copy(lax.rem(me_t + 2 * step, frames)).wait_send()

    def own_left():
        for k in range(2, trk_n, 2):
            g_copy(lax.rem(me_t + k, trk_n), me_t).wait_send()

    if always:
        own_left()
    else:
        pl.when(me_t < frames)(own_left)


def on_device(mesh_sizes, tokens, visible, virtual, *weights):
    trk_n, frm_n = mesh_sizes
    tracks, frames, width = tokens.shape
    virt = virtual.shape[0]
    assert trk_n >= frames and trk_n % 2 == 0 and frames % 2 == 0 and tracks % frm_n == 0
    assert width == 3 * LANES and HEADS == 8
    share, span = tracks // frm_n, frm_n * frames
    all_rows, virt_all = tracks * frames, virt * frames
    dma = pltpu.SemaphoreType.DMA
    vmem = pl.BlockSpec(memory_space=pltpu.VMEM)
    hbm = pl.BlockSpec(memory_space=pltpu.HBM)
    scratch = [pltpu.VMEM(w.shape, BF16) for w in weights] + [
        pltpu.VMEM((all_rows, width), BF16),
        pltpu.VMEM((frm_n, share, frames, 3 * width), F32),
        pltpu.VMEM((frm_n, share, frames, width), F32),
        pltpu.VMEM((frm_n, share, frames, LANES), F32),
        pltpu.VMEM((all_rows, width), BF16),
        pltpu.VMEM((all_rows, width), BF16),
        pltpu.VMEM((width // LANES, all_rows, LANES), F32),
        pltpu.VMEM((width // LANES, virt_all, LANES), F32),
        pltpu.VMEM((frames, LANES), F32),
        pltpu.VMEM((frames, tracks, width), BF16),
        pltpu.VMEM((frames, HEADS, LANES), F32),
        pltpu.VMEM((trk_n, tracks, width), BF16),
        pltpu.VMEM((trk_n, HEADS, LANES), F32),
        pltpu.VMEM((virt, width), BF16),
        pltpu.VMEM((frames, virt, width), BF16),
        pltpu.VMEM((width // LANES, all_rows, LANES), F32),
        [pltpu.VMEM((all_rows, LANES), F32), pltpu.VMEM((width // LANES, all_rows, LANES), F32)],
        pltpu.VMEM((virt_all, width), BF16),
        dma((2,)),
        dma((10,)),
        dma((frm_n,)), dma((frm_n,)), dma((frm_n,)), dma((frm_n,)),
        dma((frames,)), dma((trk_n,)), dma((frames,)), dma((trk_n,)),
        dma((trk_n,)), dma((frames,)), dma((frames,)),
    ]
    tracks_out, virtual_out = pl.pallas_call(
        functools.partial(kernel, (trk_n, frm_n, tracks, frames, virt, width)),
        out_shape=(
            jax.ShapeDtypeStruct((all_rows, width), BF16),
            jax.ShapeDtypeStruct((virt_all, width), BF16),
        ),
        in_specs=[hbm, vmem, hbm] + [hbm] * 10,
        out_specs=(vmem, vmem),
        scratch_shapes=scratch,
        compiler_params=pltpu.CompilerParams(
            collective_id=0, has_side_effects=True, vmem_limit_bytes=64 * 1024 * 1024
        ),
    )(
        tokens.reshape(all_rows, width), jnp.transpose(visible), virtual.reshape(virt_all, width), *weights
    )
    return tracks_out.reshape(tokens.shape), virtual_out.reshape(virtual.shape)


def solution(mesh):
    placed = (P("trk", "frm", None), P("trk", "frm"), P(None, "frm", None)) + (P(),) * 10
    return jax.shard_map(
        functools.partial(on_device, (mesh.shape["trk"], mesh.shape["frm"])),
        mesh=mesh,
        in_specs=placed,
        out_specs=(P("trk", "frm", None), P(None, "frm", None)),
        check_vma=False,
    )
```

```python
import functools
import math

import jax
import jax.numpy as jnp
from jax import lax
from jax.experimental import pallas as pl
from jax.experimental.pallas import tpu as pltpu
from jax.sharding import PartitionSpec as P

HEADS = 8
HALF = HEADS // 2
EPS = 1e-05
NEG = -1e30
LANES = 128
PIECES = 4
BF16 = jnp.bfloat16
F32 = jnp.float32
MESH = pl.DeviceIdType.MESH


def normalize(values):
    center = jnp.mean(values, -1, keepdims=True)
    shifted = values - center
    return (shifted * lax.rsqrt(jnp.mean(shifted * shifted, -1, keepdims=True) + EPS)).astype(BF16)


def dot(a, b):
    return jnp.dot(a, b, preferred_element_type=F32)


def dot_t(a, b):
    return lax.dot_general(a, b, (((1,), (1,)), ((), ())), preferred_element_type=F32)


def iota(shape, dim):
    return lax.broadcasted_iota(jnp.int32, shape, dim)


def head_masks(rows, width):
    size = width // HEADS
    lane = iota((rows, LANES), 1)
    masks = []
    for h in range(HEADS):
        low, row = h * size, []
        for j in range(width // LANES):
            first, last = low - j * LANES, low + size - j * LANES
            if last <= 0 or first >= LANES:
                row.append(None)
            else:
                row.append(jnp.where((lane >= first) & (lane < last), 1.0, 0.0).astype(BF16))
        masks.append(row)
    return masks


def spread(width, lanes_used):
    size = width // HEADS
    row = iota((LANES, width), 0)
    low = (row & (HEADS - 1)) * size
    lane = iota((LANES, width), 1)
    return jnp.where((row < lanes_used) & (lane >= low) & (lane < low + size), 1.0, 0.0).astype(BF16)


def by_head(x, masks, group, totals=False):
    keys = x.shape[0]
    lane = iota((keys, LANES), 1)
    free = lane >= LANES // 2 if group == 0 else lane < LANES // 2
    copies = []
    for h in range(group * HALF, (group + 1) * HALF):
        tiles = []
        for j in (group, group + 1):
            m = masks[h][j]
            tile = jnp.zeros((keys, LANES), BF16)
            if m is not None:
                tile = x[:, j * LANES : (j + 1) * LANES] * m[:keys]
            if totals and j == 1:
                ones = jnp.where(free & ((lane & (HEADS - 1)) == h), 1.0, 0.0).astype(BF16)
                tile = ones if m is None else tile + ones
            tiles.append(tile)
        copies.append(jnp.concatenate(tiles, axis=1))
    return jnp.concatenate(copies, axis=0)


def attend(items, masks, scale):
    rows, keys = items[0][0].shape[0], items[0][1].shape[0]
    per = LANES // keys
    lane = iota((rows, LANES), 1)
    inside = [(lane >= i * keys) & (lane < (i + 1) * keys) for i in range(per)]
    windows = [slice(group * LANES, (group + 2) * LANES) for group in range(2)]
    scores = [
        [dot_t(q[:, windows[group]], by_head(k.astype(BF16), masks, group)) for group in range(2)]
        for q, k, _, _ in items
    ]
    all_peaks, all_terms = [], []
    for both, (_, _, _, seen) in zip(scores, items):
        peaks, halves = [], []
        for score in both:
            terms = []
            for j in range(HALF * keys // LANES):
                part = score[:, j * LANES : (j + 1) * LANES]
                if seen is not None:
                    part = jnp.where(seen > 0.5, part, NEG)
                wide = None
                for i in range(per):
                    peak = jnp.max(jnp.where(inside[i], part, -3e38), axis=1, keepdims=True)
                    peaks.append(peak)
                    wide = (
                        jnp.broadcast_to(peak, part.shape)
                        if i == 0
                        else jnp.where(inside[i], peak, wide)
                    )
                term = jnp.exp2((part - wide) * scale)
                if seen is not None:
                    term = jnp.where(seen > 0.5, term, 0.0)
                terms.append(term.astype(BF16))
            halves.append(jnp.concatenate(terms, axis=1))
        all_peaks.append(peaks)
        all_terms.append(halves)
    outs = [
        [dot(half, by_head(v.astype(BF16), masks, group, True)) for group, half in enumerate(halves)]
        for halves, (_, _, v, _) in zip(all_terms, items)
    ]
    left = lane < LANES // 2
    results = []
    for (first, second), peaks in zip(outs, all_peaks):
        middle = jnp.where(left, first[:, LANES:], second[:, :LANES])
        den = jnp.where(left, second[:, :LANES], first[:, LANES:])
        den = den + pltpu.roll(den, LANES // 2, 1)
        total = jnp.concatenate([first[:, :LANES], middle, second[:, LANES:]], axis=1)
        results.append((total, peaks, den))
    return results


def attend_rows(q, k, v, masks, scale, seen=None):
    rows = q.shape[0]
    tiles = [jnp.zeros((rows, LANES), F32) for _ in range(q.shape[1] // LANES)]
    windows = [slice(group * LANES, (group + 2) * LANES) for group in range(2)]
    scores = [dot_t(by_head(q, masks, group), k[:, windows[group]]) for group in range(2)]
    outs, inverses = [], []
    for group, score in enumerate(scores):
        if seen is not None:
            score = jnp.where(seen > 0.5, score, NEG)
        terms = jnp.exp2((score - jnp.max(score, axis=1, keepdims=True)) * scale)
        if seen is not None:
            terms = jnp.where(seen > 0.5, terms, 0.0)
        inverses.append(1.0 / jnp.sum(terms, axis=1, keepdims=True))
        outs.append(dot(terms.astype(BF16), v[:, windows[group]]))
    for group, (out, inverse) in enumerate(zip(outs, inverses)):
        for i in range(HALF):
            part = slice(i * rows, (i + 1) * rows)
            for j in (group, group + 1):
                m = masks[group * HALF + i][j]
                if m is not None:
                    piece = out[part, (j - group) * LANES : (j - group + 1) * LANES]
                    tiles[j] += piece * inverse[part] * m[:rows].astype(F32)
    return jnp.concatenate(tiles, axis=1).astype(BF16)


def divide(sums, denominator, spreader):
    inverse = 1.0 / denominator
    high = inverse.astype(BF16).astype(F32)
    lane = iota(inverse.shape, 1)
    split = jnp.where(lane < HEADS, high, inverse - high).astype(BF16)
    return (sums * dot(split, spreader)).astype(BF16)


def put(ref, rows, values):
    for j in range(ref.shape[0]):
        ref[j, rows, :] = values[:, j * LANES : (j + 1) * LANES]


def take(ref, rows):
    return jnp.concatenate([ref[j, rows, :] for j in range(ref.shape[0])], axis=1)


def kernel(
    sizes,
    tokens_hbm, visible_ref, virtual_hbm, *rest,
):
    trk_n, frm_n, tracks, frames, virt, width = sizes
    weights_hbm = rest[:10]
    tracks_hbm, virtual_out_hbm = rest[10:12]
    weights = rest[12:22]
    (
        turned, qkv, sums, dens, back_in, updated, upd_rows, virt_rows, seen_all,
        send_rows, send_seen, got_rows, got_seen, mine, gathered, back_query, virt_flat,
        virtual_ref, x_sem, w_sem, a_send, a_recv, b_send, b_recv, s_send, s_recv, t_send, t_recv, g_send, g_recv, p_send,
    ) = rest[22:]
    time_qkv, time_out, virt_q, virt_kv, virt_out, self_qkv, self_out, back_q, back_kv, back_out = weights
    scale = (width // HEADS) ** (-0.5) * math.log2(math.e)
    me_t = lax.axis_index("trk")
    me_f = lax.axis_index("frm")
    share = tracks // frm_n
    block = share * frames
    span = frm_n * frames
    always = trk_n == frames

    loads = [
        pltpu.make_async_copy(weights_hbm[j], weights[j], w_sem.at[j]) for j in range(10)
    ]
    load_virtual = pltpu.make_async_copy(virtual_hbm, virtual_ref, x_sem.at[0])
    load_virtual.start()
    for j in (2, 0, 1, 3, 7, 4, 5, 6, 8, 9):
        loads[j].start()

    barrier = pltpu.get_barrier_semaphore()
    for k in range(1, frm_n):
        pl.semaphore_signal(
            barrier, inc=1, device_id=(me_t, lax.rem(me_f + k, frm_n)), device_id_type=MESH
        )
    for k in range(1, trk_n):
        pl.semaphore_signal(
            barrier, inc=1, device_id=(lax.rem(me_t + k, trk_n), me_f), device_id_type=MESH
        )

    mask = head_masks(max(virt, tracks, span), width)
    spread2 = spread(width, 2 * HEADS)

    pl.semaphore_wait(barrier, frm_n + trk_n - 2)

    def rows(index):
        return pl.ds(pl.multiple_of(index * block, block), block)

    def a_copy(k, peer, source):
        return pltpu.make_async_remote_copy(
            src_ref=tokens_hbm.at[rows(peer)],
            dst_ref=turned.at[rows(source)],
            send_sem=a_send.at[peer],
            recv_sem=a_recv.at[source],
            device_id=(me_t, peer),
            device_id_type=MESH,
        )

    def b_copy(peer, source):
        return pltpu.make_async_remote_copy(
            src_ref=back_in.at[rows(peer)],
            dst_ref=updated.at[rows(source)],
            send_sem=b_send.at[peer],
            recv_sem=b_recv.at[source],
            device_id=(me_t, peer),
            device_id_type=MESH,
        )

    def s_copy(frame, source):
        return pltpu.make_async_remote_copy(
            src_ref=send_rows.at[frame], dst_ref=got_rows.at[source],
            send_sem=s_send.at[frame], recv_sem=s_recv.at[source],
            device_id=(frame, me_f), device_id_type=MESH,
        )

    def t_copy(frame, source):
        return pltpu.make_async_remote_copy(
            src_ref=send_seen.at[frame], dst_ref=got_seen.at[source],
            send_sem=t_send.at[frame], recv_sem=t_recv.at[source],
            device_id=(frame, me_f), device_id_type=MESH,
        )

    def remote(frame, step, act):
        if always:
            if step < frames - 1:
                act()
        else:
            pl.when(frame != me_t)(act)

    own_tokens = pltpu.make_async_copy(
        tokens_hbm.at[rows(me_f)], turned.at[rows(me_f)], x_sem.at[1]
    )
    for k in range(1, frm_n):
        a_copy(k, lax.rem(me_f + k, frm_n), me_f).start()
    own_tokens.start()

    loads[2].wait()
    every = slice(None)
    load_virtual.wait()
    virtual = virtual_ref[...].astype(F32)
    put(virt_rows, every, virtual)
    own = lax.rem(me_t, frames)
    rows_here = take(virt_rows, pl.ds(own, virt, stride=frames))
    virt_query = dot(normalize(rows_here), virt_q[...]).astype(BF16)
    repeat = jnp.where(
        iota((tracks, LANES), 0) == lax.rem(iota((tracks, LANES), 1), tracks), 1.0, 0.0
    ).astype(BF16)
    seen_all[...] = dot(visible_ref[...].astype(F32).astype(BF16), repeat)
    for step in range(frames):
        frame = lax.rem(me_t + 1 + step, frames)
        send_seen[frame] = jnp.broadcast_to(seen_all[pl.ds(frame, 1), :], (HEADS, LANES))
        remote(frame, step, lambda: t_copy(frame, me_t).start())
    loads[0].wait()
    own_tokens.wait()
    for k in range(1, frm_n):
        peer = lax.rem(me_f + frm_n - k, frm_n)
        a_copy(k, peer, peer).wait_recv()

    qkv[...] = dot(normalize(turned[...].astype(F32)), time_qkv[...]).reshape(
        frm_n, share, frames, 3 * width
    )
    items = []
    for n in range(share):
        track = qkv[:, n].reshape(span, 3 * width)
        items.append(
            (track[:, :width].astype(BF16), track[:, width : 2 * width], track[:, 2 * width :], None)
        )
    for n, (total, _, den) in enumerate(attend(items, mask, scale)):
        sums[:, n] = total.reshape(frm_n, frames, width)
        dens[:, n] = den.reshape(frm_n, frames, LANES)
    all_rows = tracks * frames
    mixed = divide(
        sums[...].reshape(all_rows, width), dens[...].reshape(all_rows, LANES), spread2
    )
    loads[1].wait()
    back_in[...] = (turned[...].astype(F32) + dot(mixed, time_out[...])).astype(BF16)
    for k in range(1, frm_n):
        b_copy(lax.rem(me_f + k, frm_n), me_f).start()
    updated[rows(me_f), :] = back_in[rows(me_f), :]
    loads[3].wait()
    loads[7].wait()
    for k in range(1, frm_n):
        peer = lax.rem(me_f + frm_n - k, frm_n)
        b_copy(peer, peer).wait_recv()

    now = updated[...].astype(F32)
    put(upd_rows, every, now)
    for step in range(frames):
        frame = lax.rem(me_t + 1 + step, frames)
        send_rows[frame] = take(upd_rows, pl.ds(frame, tracks, stride=frames)).astype(BF16)
        remote(frame, step, lambda: s_copy(frame, me_t).start())
    fresh = normalize(now)
    put(back_query, every, dot(fresh, back_q[...]))
    loads[4].wait()
    loads[5].wait()
    loads[6].wait()

    side = lax.rem(me_t, 2)
    partner = me_t + 1 - 2 * side

    def g_copy(peer, frame):
        return pltpu.make_async_remote_copy(
            src_ref=mine, dst_ref=gathered.at[frame],
            send_sem=g_send.at[peer], recv_sem=g_recv.at[frame],
            device_id=(peer, me_f), device_id_type=MESH,
        )

    def p_copy(frame):
        return pltpu.make_async_remote_copy(
            src_ref=gathered.at[frame], dst_ref=gathered.at[frame],
            send_sem=p_send.at[frame], recv_sem=g_recv.at[frame],
            device_id=(partner, me_f), device_id_type=MESH,
        )

    def own_or(frame, step, own, other):
        if always:
            own() if step == 0 else other()
        else:
            pl.when(frame == me_t)(own)
            pl.when(frame != me_t)(other)

    def own_frame():
        got_rows[me_t] = send_rows[me_t]
        got_seen[me_t] = send_seen[me_t]
        sources = [lax.rem(me_t + trk_n - k, trk_n) for k in range(trk_n)]
        for peer in sources[1:]:
            t_copy(me_t, peer).wait_recv()
        lane = iota((1, LANES), 1)
        per = LANES // tracks
        seen = []
        for j in range(0, trk_n, per):
            tile = got_seen[sources[j], :1, :]
            for i in range(1, per):
                tile = jnp.where(lane >= i * tracks, got_seen[sources[j + i], :1, :], tile)
            seen.append(tile)
        seen = jnp.concatenate(seen, axis=1)
        parts = []
        for start in (0, trk_n // 2):
            some = sources[start : start + trk_n // 2]
            for peer in some:
                if start > 0 or peer is not sources[0]:
                    s_copy(me_t, peer).wait_recv()
            arrived = jnp.concatenate([got_rows[peer].astype(F32) for peer in some], axis=0)
            parts.append(dot(normalize(arrived), virt_kv[...]).astype(BF16))
        pair = jnp.concatenate(parts, axis=0)
        attended = attend_rows(
            virt_query, pair[:, :width], pair[:, width:], mask, scale, seen
        )
        cross = (rows_here + dot(attended, virt_out[...])).astype(BF16).astype(F32)
        proj = dot(normalize(cross), self_qkv[...])
        proj = proj.astype(BF16)
        self_mixed = attend_rows(
            proj[:, :width], proj[:, width : 2 * width], proj[:, 2 * width :], mask, scale
        )
        mine[...] = (cross + dot(self_mixed, self_out[...])).astype(BF16)
        for k in range(2, trk_n, 2):
            g_copy(lax.rem(me_t + k, trk_n), me_t).start()
        gathered[me_t] = mine[...]

    if always:
        own_frame()
    else:
        pl.when(me_t < frames)(own_frame)

    loads[8].wait()
    loads[9].wait()
    dens_flat, sums_flat = virt_flat

    def back(order):
        rows_f = [gathered[frame].astype(F32) for frame in order]
        for frame, values in zip(order, rows_f):
            put(virt_rows, pl.ds(frame, virt, stride=frames), values)
        both = dot(normalize(jnp.concatenate(rows_f, axis=0)), back_kv[...])
        items = []
        for j, frame in enumerate(order):
            query = take(back_query, pl.ds(frame, tracks, stride=frames)).astype(BF16)
            part = both[j * virt : (j + 1) * virt]
            items.append((query, part[:, :width], part[:, width:], None))
        for frame, (total, _, den) in zip(order, attend(items, mask, scale)):
            put(sums_flat, pl.ds(frame, tracks, stride=frames), total)
            dens_flat[pl.ds(frame, tracks, stride=frames), :] = den

    mine_first = [lax.rem(me_t + frames - 2 * step, frames) for step in range(frames // 2)]
    for step, frame in enumerate(mine_first):

        def arrived(frame=frame):
            g_copy(frame, frame).wait_recv()

        own_or(frame, step, lambda: None, arrived)
        p_copy(frame).start()
        if step == 0:
            back([frame])
    back(mine_first[1:])
    others = [lax.rem(partner + frames - 2 * step, frames) for step in range(frames // 2)]
    for frame in others:
        p_copy(frame).wait_recv()
    back(others)
    virtual_ref[...] = take(virt_rows, every).astype(BF16)
    store_virtual = pltpu.make_async_copy(virtual_ref, virtual_out_hbm, x_sem.at[0])
    store_virtual.start()
    back_mixed = divide(take(sums_flat, every), dens_flat[...], spread2)
    turned[...] = (updated[...].astype(F32) + dot(back_mixed, back_out[...])).astype(BF16)
    store_tracks = pltpu.make_async_copy(turned, tracks_hbm, x_sem.at[1])
    store_tracks.start()

    for k in range(1, frm_n):
        peer = lax.rem(me_f + k, frm_n)
        a_copy(k, peer, me_f).wait_send()
        b_copy(peer, me_f).wait_send()
    for step in range(frames):
        frame = lax.rem(me_t + 1 + step, frames)

        def left(frame=frame):
            s_copy(frame, me_t).wait_send()
            t_copy(frame, me_t).wait_send()

        remote(frame, step, left)

    for step in range(frames // 2):
        p_copy(lax.rem(me_t + 2 * step, frames)).wait_send()

    def own_left():
        for k in range(2, trk_n, 2):
            g_copy(lax.rem(me_t + k, trk_n), me_t).wait_send()

    if always:
        own_left()
    else:
        pl.when(me_t < frames)(own_left)

    store_virtual.wait()
    store_tracks.wait()


def hand_over(tracks_in, virtual_in, tracks_out, virtual_out, sem):
    copies = []
    for j, (source, target) in enumerate(((virtual_in, virtual_out), (tracks_in, tracks_out))):
        rows = source.shape[0] // PIECES
        for i in range(PIECES):
            part = pl.ds(i * rows, rows)
            copies.append(pltpu.make_async_copy(source.at[part], target.at[part], sem.at[j, i]))
    for copy in copies:
        copy.start()
    for copy in copies:
        copy.wait()


def on_device(mesh_sizes, tokens, visible, virtual, *weights):
    trk_n, frm_n = mesh_sizes
    tracks, frames, width = tokens.shape
    virt = virtual.shape[0]
    assert trk_n >= frames and trk_n % 2 == 0 and frames % 2 == 0 and tracks % frm_n == 0
    assert width == 3 * LANES and HEADS == 8
    share, span = tracks // frm_n, frm_n * frames
    all_rows, virt_all = tracks * frames, virt * frames
    dma = pltpu.SemaphoreType.DMA
    vmem = pl.BlockSpec(memory_space=pltpu.VMEM)
    hbm = pl.BlockSpec(memory_space=pltpu.HBM)
    scratch = [pltpu.VMEM(w.shape, BF16) for w in weights] + [
        pltpu.VMEM((all_rows, width), BF16),
        pltpu.VMEM((frm_n, share, frames, 3 * width), F32),
        pltpu.VMEM((frm_n, share, frames, width), F32),
        pltpu.VMEM((frm_n, share, frames, LANES), F32),
        pltpu.VMEM((all_rows, width), BF16),
        pltpu.VMEM((all_rows, width), BF16),
        pltpu.VMEM((width // LANES, all_rows, LANES), F32),
        pltpu.VMEM((width // LANES, virt_all, LANES), F32),
        pltpu.VMEM((frames, LANES), F32),
        pltpu.VMEM((frames, tracks, width), BF16),
        pltpu.VMEM((frames, HEADS, LANES), F32),
        pltpu.VMEM((trk_n, tracks, width), BF16),
        pltpu.VMEM((trk_n, HEADS, LANES), F32),
        pltpu.VMEM((virt, width), BF16),
        pltpu.VMEM((frames, virt, width), BF16),
        pltpu.VMEM((width // LANES, all_rows, LANES), F32),
        [pltpu.VMEM((all_rows, LANES), F32), pltpu.VMEM((width // LANES, all_rows, LANES), F32)],
        pltpu.VMEM((virt_all, width), BF16),
        dma((2,)),
        dma((10,)),
        dma((frm_n,)), dma((frm_n,)), dma((frm_n,)), dma((frm_n,)),
        dma((frames,)), dma((trk_n,)), dma((frames,)), dma((trk_n,)),
        dma((trk_n,)), dma((frames,)), dma((frames,)),
    ]
    tracks_out, virtual_out = pl.pallas_call(
        functools.partial(kernel, (trk_n, frm_n, tracks, frames, virt, width)),
        out_shape=(
            jax.ShapeDtypeStruct((all_rows, width), BF16),
            jax.ShapeDtypeStruct((virt_all, width), BF16),
        ),
        in_specs=[hbm, vmem, hbm] + [hbm] * 10,
        out_specs=(hbm, hbm),
        scratch_shapes=scratch,
        compiler_params=pltpu.CompilerParams(
            collective_id=0, has_side_effects=True, vmem_limit_bytes=60 * 1024 * 1024
        ),
    )(
        tokens.reshape(all_rows, width), jnp.transpose(visible), virtual.reshape(virt_all, width), *weights
    )
    anywhere = pl.BlockSpec(memory_space=pl.ANY)
    tracks_out, virtual_out = pl.pallas_call(
        hand_over,
        out_shape=(
            jax.ShapeDtypeStruct((all_rows, width), BF16),
            jax.ShapeDtypeStruct((virt_all, width), BF16),
        ),
        in_specs=[anywhere, anywhere],
        out_specs=(anywhere, anywhere),
        scratch_shapes=[dma((2, PIECES))],
        compiler_params=pltpu.CompilerParams(vmem_limit_bytes=60 * 1024 * 1024),
    )(tracks_out, virtual_out)
    return tracks_out.reshape(tokens.shape), virtual_out.reshape(virtual.shape)


def solution(mesh):
    placed = (P("trk", "frm", None), P("trk", "frm"), P(None, "frm", None)) + (P(),) * 10
    return jax.shard_map(
        functools.partial(on_device, (mesh.shape["trk"], mesh.shape["frm"])),
        mesh=mesh,
        in_specs=placed,
        out_specs=(P("trk", "frm", None), P(None, "frm", None)),
        check_vma=False,
    )
```

```python
import functools
import math

import jax
import jax.numpy as jnp
from jax import lax
from jax.experimental import pallas as pl
from jax.experimental.pallas import tpu as pltpu
from jax.sharding import PartitionSpec as P

HEADS = 8
HALF = HEADS // 2
EPS = 1e-05
NEG = -1e30
LANES = 128
PIECES = 2
BF16 = jnp.bfloat16
F32 = jnp.float32
MESH = pl.DeviceIdType.MESH


def normalize(values):
    center = jnp.mean(values, -1, keepdims=True)
    shifted = values - center
    return (shifted * lax.rsqrt(jnp.mean(shifted * shifted, -1, keepdims=True) + EPS)).astype(BF16)


def dot(a, b):
    return jnp.dot(a, b, preferred_element_type=F32)


def dot_t(a, b):
    return lax.dot_general(a, b, (((1,), (1,)), ((), ())), preferred_element_type=F32)


def iota(shape, dim):
    return lax.broadcasted_iota(jnp.int32, shape, dim)


def head_masks(rows, width):
    size = width // HEADS
    lane = iota((rows, LANES), 1)
    masks = []
    for h in range(HEADS):
        low, row = h * size, []
        for j in range(width // LANES):
            first, last = low - j * LANES, low + size - j * LANES
            if last <= 0 or first >= LANES:
                row.append(None)
            else:
                row.append(jnp.where((lane >= first) & (lane < last), 1.0, 0.0).astype(BF16))
        masks.append(row)
    return masks


def spread(width, lanes_used):
    size = width // HEADS
    row = iota((LANES, width), 0)
    low = (row & (HEADS - 1)) * size
    lane = iota((LANES, width), 1)
    return jnp.where((row < lanes_used) & (lane >= low) & (lane < low + size), 1.0, 0.0).astype(BF16)


def by_head(x, masks, group, totals=False):
    keys = x.shape[0]
    lane = iota((keys, LANES), 1)
    free = lane >= LANES // 2 if group == 0 else lane < LANES // 2
    copies = []
    for h in range(group * HALF, (group + 1) * HALF):
        tiles = []
        for j in (group, group + 1):
            m = masks[h][j]
            tile = jnp.zeros((keys, LANES), BF16)
            if m is not None:
                tile = x[:, j * LANES : (j + 1) * LANES] * m[:keys]
            if totals and j == 1:
                ones = jnp.where(free & ((lane & (HEADS - 1)) == h), 1.0, 0.0).astype(BF16)
                tile = ones if m is None else tile + ones
            tiles.append(tile)
        copies.append(jnp.concatenate(tiles, axis=1))
    return jnp.concatenate(copies, axis=0)


def attend(items, masks, scale):
    rows, keys = items[0][0].shape[0], items[0][1].shape[0]
    per = LANES // keys
    lane = iota((rows, LANES), 1)
    inside = [(lane >= i * keys) & (lane < (i + 1) * keys) for i in range(per)]
    windows = [slice(group * LANES, (group + 2) * LANES) for group in range(2)]
    scores = [
        [dot_t(q[:, windows[group]], by_head(k.astype(BF16), masks, group)) for group in range(2)]
        for q, k, _, _ in items
    ]
    all_peaks, all_terms = [], []
    for both, (_, _, _, seen) in zip(scores, items):
        peaks, halves = [], []
        for score in both:
            terms = []
            for j in range(HALF * keys // LANES):
                part = score[:, j * LANES : (j + 1) * LANES]
                if seen is not None:
                    part = jnp.where(seen > 0.5, part, NEG)
                wide = None
                for i in range(per):
                    peak = jnp.max(jnp.where(inside[i], part, -3e38), axis=1, keepdims=True)
                    peaks.append(peak)
                    wide = (
                        jnp.broadcast_to(peak, part.shape)
                        if i == 0
                        else jnp.where(inside[i], peak, wide)
                    )
                term = jnp.exp2((part - wide) * scale)
                if seen is not None:
                    term = jnp.where(seen > 0.5, term, 0.0)
                terms.append(term.astype(BF16))
            halves.append(jnp.concatenate(terms, axis=1))
        all_peaks.append(peaks)
        all_terms.append(halves)
    outs = [
        [dot(half, by_head(v.astype(BF16), masks, group, True)) for group, half in enumerate(halves)]
        for halves, (_, _, v, _) in zip(all_terms, items)
    ]
    left = lane < LANES // 2
    results = []
    for (first, second), peaks in zip(outs, all_peaks):
        middle = jnp.where(left, first[:, LANES:], second[:, :LANES])
        den = jnp.where(left, second[:, :LANES], first[:, LANES:])
        den = den + pltpu.roll(den, LANES // 2, 1)
        total = jnp.concatenate([first[:, :LANES], middle, second[:, LANES:]], axis=1)
        results.append((total, peaks, den))
    return results


def attend_rows(q, k, v, masks, scale, seen=None):
    rows = q.shape[0]
    tiles = [jnp.zeros((rows, LANES), F32) for _ in range(q.shape[1] // LANES)]
    windows = [slice(group * LANES, (group + 2) * LANES) for group in range(2)]
    scores = [dot_t(by_head(q, masks, group), k[:, windows[group]]) for group in range(2)]
    outs, inverses = [], []
    for group, score in enumerate(scores):
        if seen is not None:
            score = jnp.where(seen > 0.5, score, NEG)
        terms = jnp.exp2((score - jnp.max(score, axis=1, keepdims=True)) * scale)
        if seen is not None:
            terms = jnp.where(seen > 0.5, terms, 0.0)
        inverses.append(1.0 / jnp.sum(terms, axis=1, keepdims=True))
        outs.append(dot(terms.astype(BF16), v[:, windows[group]]))
    for group, (out, inverse) in enumerate(zip(outs, inverses)):
        for i in range(HALF):
            part = slice(i * rows, (i + 1) * rows)
            for j in (group, group + 1):
                m = masks[group * HALF + i][j]
                if m is not None:
                    piece = out[part, (j - group) * LANES : (j - group + 1) * LANES]
                    tiles[j] += piece * inverse[part] * m[:rows].astype(F32)
    return jnp.concatenate(tiles, axis=1).astype(BF16)


def divide(sums, denominator, spreader):
    inverse = 1.0 / denominator
    high = inverse.astype(BF16).astype(F32)
    lane = iota(inverse.shape, 1)
    split = jnp.where(lane < HEADS, high, inverse - high).astype(BF16)
    return (sums * dot(split, spreader)).astype(BF16)


def put(ref, rows, values):
    for j in range(ref.shape[0]):
        ref[j, rows, :] = values[:, j * LANES : (j + 1) * LANES]


def take(ref, rows):
    return jnp.concatenate([ref[j, rows, :] for j in range(ref.shape[0])], axis=1)


def kernel(
    sizes,
    tokens_hbm, visible_ref, virtual_hbm, *rest,
):
    trk_n, frm_n, tracks, frames, virt, width = sizes
    weights_hbm = rest[:10]
    tracks_hbm, virtual_out_hbm = rest[10:12]
    weights = rest[12:22]
    (
        turned, qkv, sums, dens, back_in, updated, upd_rows, virt_rows, seen_all,
        send_rows, send_seen, got_rows, got_seen, mine, gathered, back_query, virt_flat,
        virtual_ref, x_sem, w_sem, a_send, a_recv, b_send, b_recv, s_send, s_recv, t_send, t_recv, g_send, g_recv, p_send,
    ) = rest[22:]
    time_qkv, time_out, virt_q, virt_kv, virt_out, self_qkv, self_out, back_q, back_kv, back_out = weights
    scale = (width // HEADS) ** (-0.5) * math.log2(math.e)
    me_t = lax.axis_index("trk")
    me_f = lax.axis_index("frm")
    share = tracks // frm_n
    block = share * frames
    span = frm_n * frames
    always = trk_n == frames

    loads = [
        pltpu.make_async_copy(weights_hbm[j], weights[j], w_sem.at[j]) for j in range(10)
    ]
    load_virtual = pltpu.make_async_copy(virtual_hbm, virtual_ref, x_sem.at[0])
    load_virtual.start()
    for j in (2, 0, 1, 3, 7, 4, 5, 6, 8, 9):
        loads[j].start()

    barrier = pltpu.get_barrier_semaphore()
    for k in range(1, frm_n):
        pl.semaphore_signal(
            barrier, inc=1, device_id=(me_t, lax.rem(me_f + k, frm_n)), device_id_type=MESH
        )
    for k in range(1, trk_n):
        pl.semaphore_signal(
            barrier, inc=1, device_id=(lax.rem(me_t + k, trk_n), me_f), device_id_type=MESH
        )

    mask = head_masks(max(virt, tracks, span), width)
    spread2 = spread(width, 2 * HEADS)

    pl.semaphore_wait(barrier, frm_n + trk_n - 2)

    def rows(index):
        return pl.ds(pl.multiple_of(index * block, block), block)

    def a_copy(k, peer, source):
        return pltpu.make_async_remote_copy(
            src_ref=tokens_hbm.at[rows(peer)],
            dst_ref=turned.at[rows(source)],
            send_sem=a_send.at[peer],
            recv_sem=a_recv.at[source],
            device_id=(me_t, peer),
            device_id_type=MESH,
        )

    def b_copy(peer, source):
        return pltpu.make_async_remote_copy(
            src_ref=back_in.at[rows(peer)],
            dst_ref=updated.at[rows(source)],
            send_sem=b_send.at[peer],
            recv_sem=b_recv.at[source],
            device_id=(me_t, peer),
            device_id_type=MESH,
        )

    def s_copy(frame, source):
        return pltpu.make_async_remote_copy(
            src_ref=send_rows.at[frame], dst_ref=got_rows.at[source],
            send_sem=s_send.at[frame], recv_sem=s_recv.at[source],
            device_id=(frame, me_f), device_id_type=MESH,
        )

    def t_copy(frame, source):
        return pltpu.make_async_remote_copy(
            src_ref=send_seen.at[frame], dst_ref=got_seen.at[source],
            send_sem=t_send.at[frame], recv_sem=t_recv.at[source],
            device_id=(frame, me_f), device_id_type=MESH,
        )

    def remote(frame, step, act):
        if always:
            if step < frames - 1:
                act()
        else:
            pl.when(frame != me_t)(act)

    own_tokens = pltpu.make_async_copy(
        tokens_hbm.at[rows(me_f)], turned.at[rows(me_f)], x_sem.at[1]
    )
    for k in range(1, frm_n):
        a_copy(k, lax.rem(me_f + k, frm_n), me_f).start()
    own_tokens.start()

    loads[2].wait()
    every = slice(None)
    load_virtual.wait()
    virtual = virtual_ref[...].astype(F32)
    put(virt_rows, every, virtual)
    own = lax.rem(me_t, frames)
    rows_here = take(virt_rows, pl.ds(own, virt, stride=frames))
    virt_query = dot(normalize(rows_here), virt_q[...]).astype(BF16)
    repeat = jnp.where(
        iota((tracks, LANES), 0) == lax.rem(iota((tracks, LANES), 1), tracks), 1.0, 0.0
    ).astype(BF16)
    seen_all[...] = dot(visible_ref[...].astype(F32).astype(BF16), repeat)
    for step in range(frames):
        frame = lax.rem(me_t + 1 + step, frames)
        send_seen[frame] = jnp.broadcast_to(seen_all[pl.ds(frame, 1), :], (HEADS, LANES))
        remote(frame, step, lambda: t_copy(frame, me_t).start())
    loads[0].wait()
    own_tokens.wait()
    for k in range(1, frm_n):
        peer = lax.rem(me_f + frm_n - k, frm_n)
        a_copy(k, peer, peer).wait_recv()

    qkv[...] = dot(normalize(turned[...].astype(F32)), time_qkv[...]).reshape(
        frm_n, share, frames, 3 * width
    )
    items = []
    for n in range(share):
        track = qkv[:, n].reshape(span, 3 * width)
        items.append(
            (track[:, :width].astype(BF16), track[:, width : 2 * width], track[:, 2 * width :], None)
        )
    for n, (total, _, den) in enumerate(attend(items, mask, scale)):
        sums[:, n] = total.reshape(frm_n, frames, width)
        dens[:, n] = den.reshape(frm_n, frames, LANES)
    all_rows = tracks * frames
    mixed = divide(
        sums[...].reshape(all_rows, width), dens[...].reshape(all_rows, LANES), spread2
    )
    loads[1].wait()
    back_in[...] = (turned[...].astype(F32) + dot(mixed, time_out[...])).astype(BF16)
    for k in range(1, frm_n):
        b_copy(lax.rem(me_f + k, frm_n), me_f).start()
    updated[rows(me_f), :] = back_in[rows(me_f), :]
    loads[3].wait()
    loads[7].wait()
    for k in range(1, frm_n):
        peer = lax.rem(me_f + frm_n - k, frm_n)
        b_copy(peer, peer).wait_recv()

    now = updated[...].astype(F32)
    put(upd_rows, every, now)
    for step in range(frames):
        frame = lax.rem(me_t + 1 + step, frames)
        send_rows[frame] = take(upd_rows, pl.ds(frame, tracks, stride=frames)).astype(BF16)
        remote(frame, step, lambda: s_copy(frame, me_t).start())
    fresh = normalize(now)
    put(back_query, every, dot(fresh, back_q[...]))
    loads[4].wait()
    loads[5].wait()
    loads[6].wait()

    side = lax.rem(me_t, 2)
    partner = me_t + 1 - 2 * side

    def g_copy(peer, frame):
        return pltpu.make_async_remote_copy(
            src_ref=mine, dst_ref=gathered.at[frame],
            send_sem=g_send.at[peer], recv_sem=g_recv.at[frame],
            device_id=(peer, me_f), device_id_type=MESH,
        )

    def p_copy(frame):
        return pltpu.make_async_remote_copy(
            src_ref=gathered.at[frame], dst_ref=gathered.at[frame],
            send_sem=p_send.at[frame], recv_sem=g_recv.at[frame],
            device_id=(partner, me_f), device_id_type=MESH,
        )

    def own_or(frame, step, own, other):
        if always:
            own() if step == 0 else other()
        else:
            pl.when(frame == me_t)(own)
            pl.when(frame != me_t)(other)

    def own_frame():
        got_rows[me_t] = send_rows[me_t]
        got_seen[me_t] = send_seen[me_t]
        sources = [lax.rem(me_t + trk_n - k, trk_n) for k in range(trk_n)]
        for peer in sources[1:]:
            t_copy(me_t, peer).wait_recv()
        lane = iota((1, LANES), 1)
        per = LANES // tracks
        seen = []
        for j in range(0, trk_n, per):
            tile = got_seen[sources[j], :1, :]
            for i in range(1, per):
                tile = jnp.where(lane >= i * tracks, got_seen[sources[j + i], :1, :], tile)
            seen.append(tile)
        seen = jnp.concatenate(seen, axis=1)
        parts = []
        for start in (0, trk_n // 2):
            some = sources[start : start + trk_n // 2]
            for peer in some:
                if start > 0 or peer is not sources[0]:
                    s_copy(me_t, peer).wait_recv()
            arrived = jnp.concatenate([got_rows[peer].astype(F32) for peer in some], axis=0)
            parts.append(dot(normalize(arrived), virt_kv[...]).astype(BF16))
        pair = jnp.concatenate(parts, axis=0)
        attended = attend_rows(
            virt_query, pair[:, :width], pair[:, width:], mask, scale, seen
        )
        cross = (rows_here + dot(attended, virt_out[...])).astype(BF16).astype(F32)
        proj = dot(normalize(cross), self_qkv[...])
        proj = proj.astype(BF16)
        self_mixed = attend_rows(
            proj[:, :width], proj[:, width : 2 * width], proj[:, 2 * width :], mask, scale
        )
        mine[...] = (cross + dot(self_mixed, self_out[...])).astype(BF16)
        for k in range(2, trk_n, 2):
            g_copy(lax.rem(me_t + k, trk_n), me_t).start()
        gathered[me_t] = mine[...]

    if always:
        own_frame()
    else:
        pl.when(me_t < frames)(own_frame)

    loads[8].wait()
    loads[9].wait()
    dens_flat, sums_flat = virt_flat

    def back(order):
        rows_f = [gathered[frame].astype(F32) for frame in order]
        for frame, values in zip(order, rows_f):
            put(virt_rows, pl.ds(frame, virt, stride=frames), values)
        both = dot(normalize(jnp.concatenate(rows_f, axis=0)), back_kv[...])
        items = []
        for j, frame in enumerate(order):
            query = take(back_query, pl.ds(frame, tracks, stride=frames)).astype(BF16)
            part = both[j * virt : (j + 1) * virt]
            items.append((query, part[:, :width], part[:, width:], None))
        for frame, (total, _, den) in zip(order, attend(items, mask, scale)):
            put(sums_flat, pl.ds(frame, tracks, stride=frames), total)
            dens_flat[pl.ds(frame, tracks, stride=frames), :] = den

    mine_first = [lax.rem(me_t + frames - 2 * step, frames) for step in range(frames // 2)]
    for step, frame in enumerate(mine_first):

        def arrived(frame=frame):
            g_copy(frame, frame).wait_recv()

        own_or(frame, step, lambda: None, arrived)
        p_copy(frame).start()
        if step == 0:
            back([frame])
    others = [lax.rem(partner + frames - 2 * step, frames) for step in range(frames // 2)]
    p_copy(others[0]).wait_recv()
    back(mine_first[1:] + others[:1])
    for frame in others[1:]:
        p_copy(frame).wait_recv()
    back(others[1:])
    virtual_ref[...] = take(virt_rows, every).astype(BF16)
    store_virtual = pltpu.make_async_copy(virtual_ref, virtual_out_hbm, x_sem.at[0])
    store_virtual.start()
    back_mixed = divide(take(sums_flat, every), dens_flat[...], spread2)
    turned[...] = (updated[...].astype(F32) + dot(back_mixed, back_out[...])).astype(BF16)
    store_tracks = pltpu.make_async_copy(turned, tracks_hbm, x_sem.at[1])
    store_tracks.start()

    for k in range(1, frm_n):
        peer = lax.rem(me_f + k, frm_n)
        a_copy(k, peer, me_f).wait_send()
        b_copy(peer, me_f).wait_send()
    for step in range(frames):
        frame = lax.rem(me_t + 1 + step, frames)

        def left(frame=frame):
            s_copy(frame, me_t).wait_send()
            t_copy(frame, me_t).wait_send()

        remote(frame, step, left)

    for step in range(frames // 2):
        p_copy(lax.rem(me_t + 2 * step, frames)).wait_send()

    def own_left():
        for k in range(2, trk_n, 2):
            g_copy(lax.rem(me_t + k, trk_n), me_t).wait_send()

    if always:
        own_left()
    else:
        pl.when(me_t < frames)(own_left)

    store_virtual.wait()
    store_tracks.wait()


def hand_over(tracks_in, virtual_in, tracks_out, virtual_out, tracks_held, virtual_held, sem):
    ways = ((virtual_in, virtual_held, virtual_out), (tracks_in, tracks_held, tracks_out))
    into, onward = [], []
    for j, (source, held, target) in enumerate(ways):
        rows = source.shape[0] // PIECES
        for i in range(PIECES):
            part = pl.ds(i * rows, rows)
            into.append(pltpu.make_async_copy(source.at[part], held.at[part], sem.at[0, j, i]))
            onward.append(pltpu.make_async_copy(held.at[part], target.at[part], sem.at[1, j, i]))
    for copy in into:
        copy.start()
    for copy, following in zip(into, onward):
        copy.wait()
        following.start()
    for copy in onward:
        copy.wait()


def on_device(mesh_sizes, tokens, visible, virtual, *weights):
    trk_n, frm_n = mesh_sizes
    tracks, frames, width = tokens.shape
    virt = virtual.shape[0]
    assert trk_n >= frames and trk_n % 2 == 0 and frames % 2 == 0 and tracks % frm_n == 0
    assert width == 3 * LANES and HEADS == 8
    share, span = tracks // frm_n, frm_n * frames
    all_rows, virt_all = tracks * frames, virt * frames
    dma = pltpu.SemaphoreType.DMA
    vmem = pl.BlockSpec(memory_space=pltpu.VMEM)
    hbm = pl.BlockSpec(memory_space=pltpu.HBM)
    scratch = [pltpu.VMEM(w.shape, BF16) for w in weights] + [
        pltpu.VMEM((all_rows, width), BF16),
        pltpu.VMEM((frm_n, share, frames, 3 * width), F32),
        pltpu.VMEM((frm_n, share, frames, width), F32),
        pltpu.VMEM((frm_n, share, frames, LANES), F32),
        pltpu.VMEM((all_rows, width), BF16),
        pltpu.VMEM((all_rows, width), BF16),
        pltpu.VMEM((width // LANES, all_rows, LANES), F32),
        pltpu.VMEM((width // LANES, virt_all, LANES), F32),
        pltpu.VMEM((frames, LANES), F32),
        pltpu.VMEM((frames, tracks, width), BF16),
        pltpu.VMEM((frames, HEADS, LANES), F32),
        pltpu.VMEM((trk_n, tracks, width), BF16),
        pltpu.VMEM((trk_n, HEADS, LANES), F32),
        pltpu.VMEM((virt, width), BF16),
        pltpu.VMEM((frames, virt, width), BF16),
        pltpu.VMEM((width // LANES, all_rows, LANES), F32),
        [pltpu.VMEM((all_rows, LANES), F32), pltpu.VMEM((width // LANES, all_rows, LANES), F32)],
        pltpu.VMEM((virt_all, width), BF16),
        dma((2,)),
        dma((10,)),
        dma((frm_n,)), dma((frm_n,)), dma((frm_n,)), dma((frm_n,)),
        dma((frames,)), dma((trk_n,)), dma((frames,)), dma((trk_n,)),
        dma((trk_n,)), dma((frames,)), dma((frames,)),
    ]
    tracks_out, virtual_out = pl.pallas_call(
        functools.partial(kernel, (trk_n, frm_n, tracks, frames, virt, width)),
        out_shape=(
            jax.ShapeDtypeStruct((all_rows, width), BF16),
            jax.ShapeDtypeStruct((virt_all, width), BF16),
        ),
        in_specs=[hbm, vmem, hbm] + [hbm] * 10,
        out_specs=(hbm, hbm),
        scratch_shapes=scratch,
        compiler_params=pltpu.CompilerParams(
            collective_id=0, has_side_effects=True, vmem_limit_bytes=60 * 1024 * 1024
        ),
    )(
        tokens.reshape(all_rows, width), jnp.transpose(visible), virtual.reshape(virt_all, width), *weights
    )
    anywhere = pl.BlockSpec(memory_space=pl.ANY)
    tracks_out, virtual_out = pl.pallas_call(
        hand_over,
        out_shape=(
            jax.ShapeDtypeStruct((all_rows, width), BF16),
            jax.ShapeDtypeStruct((virt_all, width), BF16),
        ),
        in_specs=[anywhere, anywhere],
        out_specs=(anywhere, anywhere),
        scratch_shapes=[
            pltpu.VMEM((all_rows, width), BF16), pltpu.VMEM((virt_all, width), BF16),
            dma((2, 2, PIECES)),
        ],
        compiler_params=pltpu.CompilerParams(vmem_limit_bytes=60 * 1024 * 1024),
    )(tracks_out, virtual_out)
    return tracks_out.reshape(tokens.shape), virtual_out.reshape(virtual.shape)


def solution(mesh):
    placed = (P("trk", "frm", None), P("trk", "frm"), P(None, "frm", None)) + (P(),) * 10
    return jax.shard_map(
        functools.partial(on_device, (mesh.shape["trk"], mesh.shape["frm"])),
        mesh=mesh,
        in_specs=placed,
        out_specs=(P("trk", "frm", None), P(None, "frm", None)),
        check_vma=False,
    )
```

```python
import functools
import math

import jax
import jax.numpy as jnp
from jax import lax
from jax.experimental import pallas as pl
from jax.experimental.pallas import tpu as pltpu
from jax.sharding import PartitionSpec as P

HEADS = 8
HALF = HEADS // 2
EPS = 1e-05
NEG = -1e30
LANES = 128
PIECES = 2
BF16 = jnp.bfloat16
F32 = jnp.float32
MESH = pl.DeviceIdType.MESH


def normalize(values):
    center = jnp.mean(values, -1, keepdims=True)
    shifted = values - center
    return (shifted * lax.rsqrt(jnp.mean(shifted * shifted, -1, keepdims=True) + EPS)).astype(BF16)


def dot(a, b):
    return jnp.dot(a, b, preferred_element_type=F32)


def dot_t(a, b):
    return lax.dot_general(a, b, (((1,), (1,)), ((), ())), preferred_element_type=F32)


def iota(shape, dim):
    return lax.broadcasted_iota(jnp.int32, shape, dim)


def head_masks(rows, width):
    size = width // HEADS
    lane = iota((rows, LANES), 1)
    masks = []
    for h in range(HEADS):
        low, row = h * size, []
        for j in range(width // LANES):
            first, last = low - j * LANES, low + size - j * LANES
            if last <= 0 or first >= LANES:
                row.append(None)
            else:
                row.append(jnp.where((lane >= first) & (lane < last), 1.0, 0.0).astype(BF16))
        masks.append(row)
    return masks


def spread(width, lanes_used):
    size = width // HEADS
    row = iota((LANES, width), 0)
    low = (row & (HEADS - 1)) * size
    lane = iota((LANES, width), 1)
    return jnp.where((row < lanes_used) & (lane >= low) & (lane < low + size), 1.0, 0.0).astype(BF16)


def by_head(x, masks, group, totals=False):
    keys = x.shape[0]
    lane = iota((keys, LANES), 1)
    free = lane >= LANES // 2 if group == 0 else lane < LANES // 2
    copies = []
    for h in range(group * HALF, (group + 1) * HALF):
        tiles = []
        for j in (group, group + 1):
            m = masks[h][j]
            tile = jnp.zeros((keys, LANES), BF16)
            if m is not None:
                tile = x[:, j * LANES : (j + 1) * LANES] * m[:keys]
            if totals and j == 1:
                ones = jnp.where(free & ((lane & (HEADS - 1)) == h), 1.0, 0.0).astype(BF16)
                tile = ones if m is None else tile + ones
            tiles.append(tile)
        copies.append(jnp.concatenate(tiles, axis=1))
    return jnp.concatenate(copies, axis=0)


def attend(items, masks, scale):
    rows, keys = items[0][0].shape[0], items[0][1].shape[0]
    per = LANES // keys
    lane = iota((rows, LANES), 1)
    inside = [(lane >= i * keys) & (lane < (i + 1) * keys) for i in range(per)]
    windows = [slice(group * LANES, (group + 2) * LANES) for group in range(2)]
    scores = [
        [dot_t(q[:, windows[group]], by_head(k.astype(BF16), masks, group)) for group in range(2)]
        for q, k, _, _ in items
    ]
    all_peaks, all_terms = [], []
    for both, (_, _, _, seen) in zip(scores, items):
        peaks, halves = [], []
        for score in both:
            terms = []
            for j in range(HALF * keys // LANES):
                part = score[:, j * LANES : (j + 1) * LANES]
                if seen is not None:
                    part = jnp.where(seen > 0.5, part, NEG)
                wide = None
                for i in range(per):
                    peak = jnp.max(jnp.where(inside[i], part, -3e38), axis=1, keepdims=True)
                    peaks.append(peak)
                    wide = (
                        jnp.broadcast_to(peak, part.shape)
                        if i == 0
                        else jnp.where(inside[i], peak, wide)
                    )
                term = jnp.exp2((part - wide) * scale)
                if seen is not None:
                    term = jnp.where(seen > 0.5, term, 0.0)
                terms.append(term.astype(BF16))
            halves.append(jnp.concatenate(terms, axis=1))
        all_peaks.append(peaks)
        all_terms.append(halves)
    outs = [
        [dot(half, by_head(v.astype(BF16), masks, group, True)) for group, half in enumerate(halves)]
        for halves, (_, _, v, _) in zip(all_terms, items)
    ]
    left = lane < LANES // 2
    results = []
    for (first, second), peaks in zip(outs, all_peaks):
        middle = jnp.where(left, first[:, LANES:], second[:, :LANES])
        den = jnp.where(left, second[:, :LANES], first[:, LANES:])
        den = den + pltpu.roll(den, LANES // 2, 1)
        total = jnp.concatenate([first[:, :LANES], middle, second[:, LANES:]], axis=1)
        results.append((total, peaks, den))
    return results


def attend_rows(q, k, v, masks, scale, seen=None):
    rows = q.shape[0]
    tiles = [jnp.zeros((rows, LANES), F32) for _ in range(q.shape[1] // LANES)]
    windows = [slice(group * LANES, (group + 2) * LANES) for group in range(2)]
    scores = [dot_t(by_head(q, masks, group), k[:, windows[group]]) for group in range(2)]
    outs, inverses = [], []
    for group, score in enumerate(scores):
        if seen is not None:
            score = jnp.where(seen > 0.5, score, NEG)
        terms = jnp.exp2((score - jnp.max(score, axis=1, keepdims=True)) * scale)
        if seen is not None:
            terms = jnp.where(seen > 0.5, terms, 0.0)
        inverses.append(1.0 / jnp.sum(terms, axis=1, keepdims=True))
        outs.append(dot(terms.astype(BF16), v[:, windows[group]]))
    for group, (out, inverse) in enumerate(zip(outs, inverses)):
        for i in range(HALF):
            part = slice(i * rows, (i + 1) * rows)
            for j in (group, group + 1):
                m = masks[group * HALF + i][j]
                if m is not None:
                    piece = out[part, (j - group) * LANES : (j - group + 1) * LANES]
                    tiles[j] += piece * inverse[part] * m[:rows].astype(F32)
    return jnp.concatenate(tiles, axis=1).astype(BF16)


def divide(sums, denominator, spreader):
    inverse = 1.0 / denominator
    high = inverse.astype(BF16).astype(F32)
    lane = iota(inverse.shape, 1)
    split = jnp.where(lane < HEADS, high, inverse - high).astype(BF16)
    return (sums * dot(split, spreader)).astype(BF16)


def put(ref, rows, values):
    for j in range(ref.shape[0]):
        ref[j, rows, :] = values[:, j * LANES : (j + 1) * LANES]


def take(ref, rows):
    return jnp.concatenate([ref[j, rows, :] for j in range(ref.shape[0])], axis=1)


def kernel(
    sizes,
    tokens_hbm, visible_ref, virtual_hbm, *rest,
):
    trk_n, frm_n, tracks, frames, virt, width = sizes
    weights_hbm = rest[:10]
    tracks_hbm, virtual_out_hbm = rest[10:12]
    weights = rest[12:22]
    (
        turned, qkv, sums, dens, back_in, updated, upd_rows, virt_rows, seen_all,
        send_rows, send_seen, got_rows, got_seen, mine, gathered, back_query, virt_flat,
        virtual_ref, x_sem, w_sem, a_send, a_recv, b_send, b_recv, s_send, s_recv, t_send, t_recv, g_send, g_recv,
    ) = rest[22:]
    time_qkv, time_out, virt_q, virt_kv, virt_out, self_qkv, self_out, back_q, back_kv, back_out = weights
    scale = (width // HEADS) ** (-0.5) * math.log2(math.e)
    me_t = lax.axis_index("trk")
    me_f = lax.axis_index("frm")
    share = tracks // frm_n
    block = share * frames
    span = frm_n * frames
    always = trk_n == frames

    loads = [
        pltpu.make_async_copy(weights_hbm[j], weights[j], w_sem.at[j]) for j in range(10)
    ]
    load_virtual = pltpu.make_async_copy(virtual_hbm, virtual_ref, x_sem.at[0])
    load_virtual.start()
    for j in (2, 0, 1, 3, 7, 4, 5, 6, 8, 9):
        loads[j].start()

    barrier = pltpu.get_barrier_semaphore()
    for k in range(1, frm_n):
        pl.semaphore_signal(
            barrier, inc=1, device_id=(me_t, lax.rem(me_f + k, frm_n)), device_id_type=MESH
        )
    for k in range(1, trk_n):
        pl.semaphore_signal(
            barrier, inc=1, device_id=(lax.rem(me_t + k, trk_n), me_f), device_id_type=MESH
        )

    mask = head_masks(max(virt, tracks, span), width)
    spread2 = spread(width, 2 * HEADS)

    pl.semaphore_wait(barrier, frm_n + trk_n - 2)

    def rows(index):
        return pl.ds(pl.multiple_of(index * block, block), block)

    def a_copy(k, peer, source):
        return pltpu.make_async_remote_copy(
            src_ref=tokens_hbm.at[rows(peer)],
            dst_ref=turned.at[rows(source)],
            send_sem=a_send.at[peer],
            recv_sem=a_recv.at[source],
            device_id=(me_t, peer),
            device_id_type=MESH,
        )

    def b_copy(peer, source):
        return pltpu.make_async_remote_copy(
            src_ref=back_in.at[rows(peer)],
            dst_ref=updated.at[rows(source)],
            send_sem=b_send.at[peer],
            recv_sem=b_recv.at[source],
            device_id=(me_t, peer),
            device_id_type=MESH,
        )

    def s_copy(frame, source):
        return pltpu.make_async_remote_copy(
            src_ref=send_rows.at[frame], dst_ref=got_rows.at[source],
            send_sem=s_send.at[frame], recv_sem=s_recv.at[source],
            device_id=(frame, me_f), device_id_type=MESH,
        )

    def t_copy(frame, source):
        return pltpu.make_async_remote_copy(
            src_ref=send_seen.at[frame], dst_ref=got_seen.at[source],
            send_sem=t_send.at[frame], recv_sem=t_recv.at[source],
            device_id=(frame, me_f), device_id_type=MESH,
        )

    def remote(frame, step, act):
        if always:
            if step < frames - 1:
                act()
        else:
            pl.when(frame != me_t)(act)

    own_tokens = pltpu.make_async_copy(
        tokens_hbm.at[rows(me_f)], turned.at[rows(me_f)], x_sem.at[1]
    )
    for k in range(1, frm_n):
        a_copy(k, lax.rem(me_f + k, frm_n), me_f).start()
    own_tokens.start()

    loads[2].wait()
    every = slice(None)
    load_virtual.wait()
    virtual = virtual_ref[...].astype(F32)
    put(virt_rows, every, virtual)
    own = lax.rem(me_t, frames)
    rows_here = take(virt_rows, pl.ds(own, virt, stride=frames))
    virt_query = dot(normalize(rows_here), virt_q[...]).astype(BF16)
    repeat = jnp.where(
        iota((tracks, LANES), 0) == lax.rem(iota((tracks, LANES), 1), tracks), 1.0, 0.0
    ).astype(BF16)
    seen_all[...] = dot(visible_ref[...].astype(F32).astype(BF16), repeat)
    for step in range(frames):
        frame = lax.rem(me_t + 1 + step, frames)
        send_seen[frame] = jnp.broadcast_to(seen_all[pl.ds(frame, 1), :], (HEADS, LANES))
        remote(frame, step, lambda: t_copy(frame, me_t).start())
    loads[0].wait()
    own_tokens.wait()
    for k in range(1, frm_n):
        peer = lax.rem(me_f + frm_n - k, frm_n)
        a_copy(k, peer, peer).wait_recv()

    qkv[...] = dot(normalize(turned[...].astype(F32)), time_qkv[...]).reshape(
        frm_n, share, frames, 3 * width
    )
    items = []
    for n in range(share):
        track = qkv[:, n].reshape(span, 3 * width)
        items.append(
            (track[:, :width].astype(BF16), track[:, width : 2 * width], track[:, 2 * width :], None)
        )
    for n, (total, _, den) in enumerate(attend(items, mask, scale)):
        sums[:, n] = total.reshape(frm_n, frames, width)
        dens[:, n] = den.reshape(frm_n, frames, LANES)
    all_rows = tracks * frames
    mixed = divide(
        sums[...].reshape(all_rows, width), dens[...].reshape(all_rows, LANES), spread2
    )
    loads[1].wait()
    back_in[...] = (turned[...].astype(F32) + dot(mixed, time_out[...])).astype(BF16)
    for k in range(1, frm_n):
        b_copy(lax.rem(me_f + k, frm_n), me_f).start()
    updated[rows(me_f), :] = back_in[rows(me_f), :]
    loads[3].wait()
    loads[7].wait()
    for k in range(1, frm_n):
        peer = lax.rem(me_f + frm_n - k, frm_n)
        b_copy(peer, peer).wait_recv()

    now = updated[...].astype(F32)
    put(upd_rows, every, now)
    for step in range(frames):
        frame = lax.rem(me_t + 1 + step, frames)
        send_rows[frame] = take(upd_rows, pl.ds(frame, tracks, stride=frames)).astype(BF16)
        remote(frame, step, lambda: s_copy(frame, me_t).start())
    fresh = normalize(now)
    put(back_query, every, dot(fresh, back_q[...]))
    loads[4].wait()
    loads[5].wait()
    loads[6].wait()

    side = lax.rem(me_t, 2)
    partner = me_t + 1 - 2 * side

    def g_copy(peer, frame):
        return pltpu.make_async_remote_copy(
            src_ref=mine, dst_ref=gathered.at[frame],
            send_sem=g_send.at[peer], recv_sem=g_recv.at[frame],
            device_id=(peer, me_f), device_id_type=MESH,
        )

    def own_or(frame, step, own, other):
        if always:
            own() if step == 0 else other()
        else:
            pl.when(frame == me_t)(own)
            pl.when(frame != me_t)(other)

    def own_frame():
        got_rows[me_t] = send_rows[me_t]
        got_seen[me_t] = send_seen[me_t]
        sources = [lax.rem(me_t + trk_n - k, trk_n) for k in range(trk_n)]
        for peer in sources[1:]:
            t_copy(me_t, peer).wait_recv()
        lane = iota((1, LANES), 1)
        per = LANES // tracks
        seen = []
        for j in range(0, trk_n, per):
            tile = got_seen[sources[j], :1, :]
            for i in range(1, per):
                tile = jnp.where(lane >= i * tracks, got_seen[sources[j + i], :1, :], tile)
            seen.append(tile)
        seen = jnp.concatenate(seen, axis=1)
        parts = []
        for start in (0, trk_n // 2):
            some = sources[start : start + trk_n // 2]
            for peer in some:
                if start > 0 or peer is not sources[0]:
                    s_copy(me_t, peer).wait_recv()
            arrived = jnp.concatenate([got_rows[peer].astype(F32) for peer in some], axis=0)
            parts.append(dot(normalize(arrived), virt_kv[...]).astype(BF16))
        pair = jnp.concatenate(parts, axis=0)
        attended = attend_rows(
            virt_query, pair[:, :width], pair[:, width:], mask, scale, seen
        )
        cross = (rows_here + dot(attended, virt_out[...])).astype(BF16).astype(F32)
        proj = dot(normalize(cross), self_qkv[...])
        proj = proj.astype(BF16)
        self_mixed = attend_rows(
            proj[:, :width], proj[:, width : 2 * width], proj[:, 2 * width :], mask, scale
        )
        mine[...] = (cross + dot(self_mixed, self_out[...])).astype(BF16)
        for k in range(1, trk_n):
            g_copy(lax.rem(me_t + k, trk_n), me_t).start()
        gathered[me_t] = mine[...]

    if always:
        own_frame()
    else:
        pl.when(me_t < frames)(own_frame)

    loads[8].wait()
    loads[9].wait()
    dens_flat, sums_flat = virt_flat

    def back(order):
        rows_f = [gathered[frame].astype(F32) for frame in order]
        for frame, values in zip(order, rows_f):
            put(virt_rows, pl.ds(frame, virt, stride=frames), values)
        both = dot(normalize(jnp.concatenate(rows_f, axis=0)), back_kv[...])
        items = []
        for j, frame in enumerate(order):
            query = take(back_query, pl.ds(frame, tracks, stride=frames)).astype(BF16)
            part = both[j * virt : (j + 1) * virt]
            items.append((query, part[:, :width], part[:, width:], None))
        for frame, (total, _, den) in zip(order, attend(items, mask, scale)):
            put(sums_flat, pl.ds(frame, tracks, stride=frames), total)
            dens_flat[pl.ds(frame, tracks, stride=frames), :] = den

    mine_first = [lax.rem(me_t + frames - 2 * step, frames) for step in range(frames // 2)]
    for step, frame in enumerate(mine_first):

        def arrived(frame=frame):
            g_copy(frame, frame).wait_recv()

        own_or(frame, step, lambda: None, arrived)
        if step == 0:
            back([frame])
    others = [lax.rem(partner + frames - 2 * step, frames) for step in range(frames // 2)]
    g_copy(others[0], others[0]).wait_recv()
    back(mine_first[1:] + others[:1])
    for frame in others[1:]:
        g_copy(frame, frame).wait_recv()
    back(others[1:])
    virtual_ref[...] = take(virt_rows, every).astype(BF16)
    store_virtual = pltpu.make_async_copy(virtual_ref, virtual_out_hbm, x_sem.at[0])
    store_virtual.start()
    back_mixed = divide(take(sums_flat, every), dens_flat[...], spread2)
    turned[...] = (updated[...].astype(F32) + dot(back_mixed, back_out[...])).astype(BF16)
    store_tracks = pltpu.make_async_copy(turned, tracks_hbm, x_sem.at[1])
    store_tracks.start()

    for k in range(1, frm_n):
        peer = lax.rem(me_f + k, frm_n)
        a_copy(k, peer, me_f).wait_send()
        b_copy(peer, me_f).wait_send()
    for step in range(frames):
        frame = lax.rem(me_t + 1 + step, frames)

        def left(frame=frame):
            s_copy(frame, me_t).wait_send()
            t_copy(frame, me_t).wait_send()

        remote(frame, step, left)

    def own_left():
        for k in range(1, trk_n):
            g_copy(lax.rem(me_t + k, trk_n), me_t).wait_send()

    if always:
        own_left()
    else:
        pl.when(me_t < frames)(own_left)

    store_virtual.wait()
    store_tracks.wait()


def hand_over(tracks_in, virtual_in, tracks_out, virtual_out, tracks_held, virtual_held, sem):
    ways = ((virtual_in, virtual_held, virtual_out), (tracks_in, tracks_held, tracks_out))
    into, onward = [], []
    for j, (source, held, target) in enumerate(ways):
        rows = source.shape[0] // PIECES
        for i in range(PIECES):
            part = pl.ds(i * rows, rows)
            into.append(pltpu.make_async_copy(source.at[part], held.at[part], sem.at[0, j, i]))
            onward.append(pltpu.make_async_copy(held.at[part], target.at[part], sem.at[1, j, i]))
    for copy in into:
        copy.start()
    for copy, following in zip(into, onward):
        copy.wait()
        following.start()
    for copy in onward:
        copy.wait()


def on_device(mesh_sizes, tokens, visible, virtual, *weights):
    trk_n, frm_n = mesh_sizes
    tracks, frames, width = tokens.shape
    virt = virtual.shape[0]
    assert trk_n >= frames and trk_n % 2 == 0 and frames % 2 == 0 and tracks % frm_n == 0
    assert width == 3 * LANES and HEADS == 8
    share, span = tracks // frm_n, frm_n * frames
    all_rows, virt_all = tracks * frames, virt * frames
    dma = pltpu.SemaphoreType.DMA
    vmem = pl.BlockSpec(memory_space=pltpu.VMEM)
    hbm = pl.BlockSpec(memory_space=pltpu.HBM)
    scratch = [pltpu.VMEM(w.shape, BF16) for w in weights] + [
        pltpu.VMEM((all_rows, width), BF16),
        pltpu.VMEM((frm_n, share, frames, 3 * width), F32),
        pltpu.VMEM((frm_n, share, frames, width), F32),
        pltpu.VMEM((frm_n, share, frames, LANES), F32),
        pltpu.VMEM((all_rows, width), BF16),
        pltpu.VMEM((all_rows, width), BF16),
        pltpu.VMEM((width // LANES, all_rows, LANES), F32),
        pltpu.VMEM((width // LANES, virt_all, LANES), F32),
        pltpu.VMEM((frames, LANES), F32),
        pltpu.VMEM((frames, tracks, width), BF16),
        pltpu.VMEM((frames, HEADS, LANES), F32),
        pltpu.VMEM((trk_n, tracks, width), BF16),
        pltpu.VMEM((trk_n, HEADS, LANES), F32),
        pltpu.VMEM((virt, width), BF16),
        pltpu.VMEM((frames, virt, width), BF16),
        pltpu.VMEM((width // LANES, all_rows, LANES), F32),
        [pltpu.VMEM((all_rows, LANES), F32), pltpu.VMEM((width // LANES, all_rows, LANES), F32)],
        pltpu.VMEM((virt_all, width), BF16),
        dma((2,)),
        dma((10,)),
        dma((frm_n,)), dma((frm_n,)), dma((frm_n,)), dma((frm_n,)),
        dma((frames,)), dma((trk_n,)), dma((frames,)), dma((trk_n,)),
        dma((trk_n,)), dma((frames,)),
    ]
    tracks_out, virtual_out = pl.pallas_call(
        functools.partial(kernel, (trk_n, frm_n, tracks, frames, virt, width)),
        out_shape=(
            jax.ShapeDtypeStruct((all_rows, width), BF16),
            jax.ShapeDtypeStruct((virt_all, width), BF16),
        ),
        in_specs=[hbm, vmem, hbm] + [hbm] * 10,
        out_specs=(hbm, hbm),
        scratch_shapes=scratch,
        compiler_params=pltpu.CompilerParams(
            collective_id=0, has_side_effects=True, vmem_limit_bytes=60 * 1024 * 1024
        ),
    )(
        tokens.reshape(all_rows, width), jnp.transpose(visible), virtual.reshape(virt_all, width), *weights
    )
    anywhere = pl.BlockSpec(memory_space=pl.ANY)
    tracks_out, virtual_out = pl.pallas_call(
        hand_over,
        out_shape=(
            jax.ShapeDtypeStruct((all_rows, width), BF16),
            jax.ShapeDtypeStruct((virt_all, width), BF16),
        ),
        in_specs=[anywhere, anywhere],
        out_specs=(anywhere, anywhere),
        scratch_shapes=[
            pltpu.VMEM((all_rows, width), BF16), pltpu.VMEM((virt_all, width), BF16),
            dma((2, 2, PIECES)),
        ],
        compiler_params=pltpu.CompilerParams(vmem_limit_bytes=60 * 1024 * 1024),
    )(tracks_out, virtual_out)
    return tracks_out.reshape(tokens.shape), virtual_out.reshape(virtual.shape)


def solution(mesh):
    placed = (P("trk", "frm", None), P("trk", "frm"), P(None, "frm", None)) + (P(),) * 10
    return jax.shard_map(
        functools.partial(on_device, (mesh.shape["trk"], mesh.shape["frm"])),
        mesh=mesh,
        in_specs=placed,
        out_specs=(P("trk", "frm", None), P(None, "frm", None)),
        check_vma=False,
    )
```
